512 devices in a mesh: row: 32 (over z, x_hi), rep: 16 (over x_lo, y, core).
Axes of the slice: x: 4 (x_hi: 2, x_lo: 2; x = x_hi * 2 + x_lo), y: 4, z: 16, core: 2. Of those that a mesh axis runs over, the one named last changes fastest.
Arguments:
- features: float32 [32768, 512], P(('row', 'rep')), may hold values from -6 to 6
- weight: float32 [512, 512], replicated, may hold values from -0.25 to 0.25
- cotangent: float32 [32768, 512], P(('row', 'rep')), may hold values from -6 to 6
- tile_mask: int32 [256, 256], P('row', 'rep'), may hold values from 0 to 1
- row_codes: int32 [2, 32768], P(None, 'row'), may hold values from 1 to 32767
- col_codes: int32 [2, 32768], P(None, 'rep'), may hold values from 1 to 32767
Outputs:
- activated: float32 [32768, 512], P(('row', 'rep'))
- grad_input: float32 [32768, 512], P(('row', 'rep'))
The draws below stay inside these ranges and needn't reach their ends.
All inputs are finite; a program needn't handle non-finite values.
Results may differ from the reference program's by a relative error of at most 0.0031.
Values may be sent and summed in bfloat16 or wider, within the bound.
No kernel may reach another device: no remote copies, remote signals or barrier semaphores. Data moves between devices by JAX's collectives and lax.ppermute only.
A program may use at most 64 MiB of HBM per device.

```python
import jax
import jax.numpy as jnp
from jax import lax

F = 512
RPD = 64
TILE = 128
R = 1024
COLS = 2048
V = 32768
N_ROW = 32
N_REP = 16


def draw_tile_mask(key, part):
    key = jax.random.fold_in(key, 5)
    level_key, pick_key = jax.random.split(key)
    tile_count = V // TILE
    levels = jax.random.randint(level_key, (tile_count, 1), 3, 11)
    tile_picks = jax.random.randint(pick_key, (tile_count, tile_count), 0, 10)
    return (tile_picks < levels).astype(jnp.int32)


def with_ends(array, key, smallest, high):
    extent = array.shape
    index_at = [jax.random.randint(jax.random.fold_in(key, axis), (), 0, extent[axis]) for axis in range(len(extent))]
    array = array.at[tuple(index_at)].set(smallest)
    longest = extent.index(max(extent))
    index_at[longest] = (index_at[longest] + 1) % extent[longest]
    return array.at[tuple(index_at)].set(high)


def level_of(own_key, extent, cuts, low, top_value):
    level = 1.0
    for position, blocks in cuts:
        draws = jax.random.uniform(jax.random.fold_in(jax.random.fold_in(own_key, 6), position), (blocks,), jnp.float32, low / len(cuts), top_value / len(cuts))
        level = level * jnp.repeat(jnp.exp(draws), extent[position] // blocks).reshape((-1,) + (1,) * (len(extent) - 1 - position))
    return level


def gaussian(rng, extent, spread, reach, cuts=(), kind=jnp.bfloat16):
    result = jax.random.normal(rng, extent, jnp.float32) * spread
    if len(cuts) > 0:
        result = level_of(rng, extent, cuts, -0.22, 0.18) * result
    return jnp.clip(result, min=-reach, max=reach).astype(kind)


def setup_inputs(seed: int = 0) -> dict:
    seeds = jax.random.split(jax.random.key(seed), 7)
    return {
        "features": gaussian(seeds[0], (V, F), 1.0, 6.0, ((0, 512),), jnp.float32),
        "weight": gaussian(seeds[1], (F, F), F ** -0.5, 0.25, (), jnp.float32),
        "cotangent": gaussian(seeds[2], (V, F), 1.0, 6.0, ((0, 512),), jnp.float32),
        "tile_mask": draw_tile_mask(jax.random.fold_in(seeds[6], 71), 0),
        "row_codes": with_ends(jax.random.randint(seeds[4], (2, V), 1, 32768), jax.random.fold_in(seeds[4], 1), 1, 32767).astype(jnp.int32),
        "col_codes": with_ends(jax.random.randint(seeds[5], (2, V), 1, 32768), jax.random.fold_in(seeds[5], 1), 1, 32767).astype(jnp.int32),
    }


HIGHEST = lax.Precision.HIGHEST
hash_prime = 65521

def column_order(vertex_rows):
    row_width = vertex_rows.shape[1]
    shaped = vertex_rows.reshape(N_ROW, N_REP, RPD, row_width)
    return shaped.transpose(1, 0, 2, 3).reshape(V, row_width)

def vertex_order(column_rows):
    row_width = column_rows.shape[1]
    shaped = column_rows.reshape(N_REP, N_ROW, RPD, row_width)
    return shaped.transpose(1, 0, 2, 3).reshape(V, row_width)

def block_adjacency(tile_mask, row_codes, col_codes, block_index):
    row_start = (block_index * R).astype(jnp.int32)
    tile_start = (block_index * (R // TILE)).astype(jnp.int32)
    first_code = lax.dynamic_slice_in_dim(row_codes[0], row_start, R, 0)
    second_code = lax.dynamic_slice_in_dim(row_codes[1], row_start, R, 0)
    hashed = (first_code[:, None] * col_codes[0][None, :] + second_code[:, None] * col_codes[1][None, :]) % hash_prime
    subset = jnp.arange(V, dtype=jnp.int32) // COLS
    threshold = (10 + 20 * subset // max(N_REP - 1, 1)) * hash_prime // 1000
    kept_cells = (hashed < threshold[None, :]).astype(jnp.int32)
    rows_mask = lax.dynamic_slice_in_dim(tile_mask, tile_start, R // TILE, 0)
    tiled_mask = kept_cells.reshape(R // TILE, TILE, V // TILE, TILE) * rows_mask[:, None, :, None]
    return tiled_mask.reshape(R, V).astype(jnp.float32)

def to_low(values):
    return lax.optimization_barrier(values.astype(jnp.bfloat16)).astype(jnp.float32)

def reference(features, weight, cotangent, tile_mask, row_codes, col_codes):
    gathered = to_low(column_order(features)).reshape(N_REP, COLS, F)
    block_ids = jnp.arange(N_ROW, dtype=jnp.int32)

    def forward_block(block_index):
        adjacency = block_adjacency(tile_mask, row_codes, col_codes, block_index)
        parts = jnp.einsum('rjc,jcf->jrf', adjacency.reshape(R, N_REP, COLS), gathered, precision=HIGHEST)
        aggregate = lax.optimization_barrier(jnp.sum(parts, axis=0))
        return (aggregate, lax.optimization_barrier(jnp.sum(adjacency, axis=1)))
    aggregate, degree = lax.map(forward_block, block_ids)
    aggregate = aggregate.reshape(V, F)
    degree = degree.reshape(V)
    row_scale = lax.rsqrt(1.0 + degree)[:, None]
    hidden = (features + aggregate) * row_scale
    pre_act = jnp.dot(hidden, weight, precision=HIGHEST, preferred_element_type=jnp.float32)
    activated = jax.nn.softplus(pre_act)
    pulled = cotangent * jax.nn.sigmoid(pre_act) * row_scale
    pulled_low = to_low(pulled)

    def backward_block(running, block_index):
        adjacency = block_adjacency(tile_mask, row_codes, col_codes, block_index)
        rows_pulled = lax.dynamic_slice_in_dim(pulled_low, (block_index * R).astype(jnp.int32), R, 0)
        column_term = lax.dot_general(adjacency, rows_pulled, (((0,), (0,)), ((), ())), precision=HIGHEST, preferred_element_type=jnp.float32)
        return (running + column_term, None)
    back_sum, ignored = lax.scan(backward_block, jnp.zeros((V, F), jnp.float32), block_ids)
    total = pulled + vertex_order(back_sum)
    grad_input = lax.dot_general(total, weight, (((1,), (1,)), ((), ())), precision=HIGHEST, preferred_element_type=jnp.float32)
    return (activated, grad_input)
```

```python
import jax
import jax.numpy as jnp
from jax import lax
from jax.experimental import pallas as pl
from jax.experimental.pallas import tpu as pltpu
from jax.sharding import Mesh, PartitionSpec as P

HIGHEST = lax.Precision.HIGHEST
hash_prime = 65521
N_Z_HI, N_Z_LO, N_X_HI, N_X_LO, N_Y, N_CORE = 4, 4, 2, 2, 4, 2
N_Z = N_Z_HI * N_Z_LO
N_XY = N_X_HI * N_X_LO * N_Y
RPD = 64
F = 512
R = N_XY * RPD
COLS = N_CORE * N_Z * RPD
DIGITS = 16
AXES = ("zh", "zl", "xh", "xl", "y", "c")
XY = ("xh", "xl", "y")


def centred(value):
    residue = value % hash_prime
    return jnp.where(residue > hash_prime // 2, residue - hash_prime, residue)


def two_digits(value):
    high = (value + 128) >> 8
    return value - (high << 8), high << 8


def row_digits(first_code, second_code):
    digits = []
    for code in (first_code, second_code):
        digits.extend(two_digits(code))
        digits.extend(two_digits(centred(code << 8)))
    digits.extend(two_digits(centred((first_code + second_code) << 14)))
    digits.extend([jnp.zeros_like(first_code)] * (DIGITS - len(digits)))
    return jnp.stack(digits, axis=-1).astype(jnp.bfloat16)


def column_digits(first_code, second_code):
    digits = []
    for code in (first_code, second_code):
        low, high = two_digits(code - 16384)
        digits.extend((low, low, high >> 8, high >> 8))
    digits.extend([jnp.ones_like(first_code)] * 2)
    digits.extend([jnp.zeros_like(first_code)] * (DIGITS - len(digits)))
    return jnp.stack(digits, axis=0).astype(jnp.bfloat16)


def adjacency_kernel(left_ref, right_ref, limit_ref, adjacency_ref, degree_ref):
    value = jnp.dot(left_ref[...], right_ref[...], preferred_element_type=jnp.float32)
    residue = value - jnp.round(value * (1.0 / hash_prime)) * float(hash_prime)
    kept = jnp.logical_and(residue >= 0.0, residue < limit_ref[0])
    kept = jnp.where(kept, 1.0, 0.0)
    adjacency_ref[...] = kept.astype(jnp.bfloat16)
    degree_ref[...] = jnp.broadcast_to(jnp.sum(kept, axis=1, keepdims=True), degree_ref.shape)


def build_adjacency(left, right, limit):
    return pl.pallas_call(
        adjacency_kernel,
        grid=(N_XY,),
        in_specs=[
            pl.BlockSpec((RPD, DIGITS), lambda k: (k, 0)),
            pl.BlockSpec((DIGITS, COLS), lambda k: (0, 0)),
            pl.BlockSpec((1, 1, COLS), lambda k: (k, 0, 0)),
        ],
        out_specs=[
            pl.BlockSpec((RPD, COLS), lambda k: (k, 0)),
            pl.BlockSpec((RPD, 128), lambda k: (k, 0)),
        ],
        out_shape=[
            jax.ShapeDtypeStruct((R, COLS), jnp.bfloat16),
            jax.ShapeDtypeStruct((R, 128), jnp.float32),
        ],
        cost_estimate=pl.CostEstimate(flops=2 * R * COLS * DIGITS, bytes_accessed=2 * R * COLS, transcendentals=0),
    )(left, right, limit)


def to_other_core(values):
    return lax.ppermute(values, "c", [(0, 1), (1, 0)])


def exchange(values, axis):
    return lax.all_to_all(values, axis, 0, 0, tiled=True)


def to_all(values, axis, count):
    return exchange(jnp.broadcast_to(values[None], (count,) + values.shape).reshape(-1, values.shape[1]), axis)


def per_device(features, weight, cotangent, tile_mask, row_codes, col_codes):
    x_hi, core = lax.axis_index("xh"), lax.axis_index("c")
    subset = (lax.axis_index("xl") * N_Y + lax.axis_index("y")) * N_CORE + core

    own_rows = lax.dynamic_index_in_dim(row_codes.reshape(2, N_XY // 2, N_CORE, RPD), core, 2, False)
    own_columns = lax.dynamic_index_in_dim(col_codes.reshape(2, N_Z_HI, N_Z_LO, N_X_HI, RPD), x_hi, 3, False)
    own_columns = own_columns.transpose(0, 2, 1, 3)
    own_mask = tile_mask.reshape(N_XY // 2, N_Z_HI, N_Z_LO).transpose(0, 2, 1)
    sizes = (own_rows.size, own_columns.size, own_mask.size)
    small = jnp.concatenate([own_rows.reshape(-1), own_columns.reshape(-1), own_mask.reshape(-1)])
    small = lax.all_gather(small, ("xh", "c"), axis=0).reshape(N_X_HI, N_CORE, -1)
    rows_all = lax.dynamic_index_in_dim(small[:, :, : sizes[0]], core, 1, False)
    rows_all = rows_all.reshape(N_X_HI, 2, N_XY // 2, RPD).transpose(1, 0, 2, 3).reshape(2, R)
    columns_all = lax.dynamic_index_in_dim(small[:, :, sizes[0] : sizes[0] + sizes[1]], x_hi, 0, False)
    columns_all = columns_all.reshape(N_CORE, 2, N_Z * RPD)
    mask_all = small[:, :, sizes[0] + sizes[1] :].reshape(N_X_HI, N_CORE, N_XY // 2, N_Z)
    mask_all = mask_all.transpose(1, 0, 2, 3).reshape(N_CORE, N_XY, N_Z)

    def own_first(values):
        return jnp.where(core == 0, values, values[::-1])

    columns_all = own_first(columns_all).transpose(1, 0, 2).reshape(2, COLS)
    mask_all = own_first(mask_all)
    subsets = jnp.stack([subset, subset ^ 1])
    threshold = (10 + 20 * subsets // 15) * hash_prime // 1000
    limit = (mask_all * threshold[:, None, None]).transpose(1, 0, 2).astype(jnp.float32)
    limit = jnp.repeat(limit.reshape(N_XY, N_CORE * N_Z), RPD, axis=1).reshape(N_XY, 1, COLS)
    left = row_digits(rows_all[0], rows_all[1])
    right = column_digits(columns_all[0], columns_all[1])

    gathered = lax.all_gather(features.astype(jnp.bfloat16), "zh", axis=0, tiled=True)
    gathered = to_all(gathered, "zl", N_Z_LO)
    other = to_other_core(gathered)
    adjacency, degree = build_adjacency(left, right, limit)
    half = COLS // 2
    aggregate = jnp.dot(adjacency[:, :half], gathered, preferred_element_type=jnp.float32)
    aggregate += jnp.dot(adjacency[:, half:], other, preferred_element_type=jnp.float32)
    sent = jnp.concatenate([aggregate, degree], axis=1).astype(jnp.float16)
    arrived = exchange(sent, XY).reshape(N_XY, RPD, F + 128).astype(jnp.float32).sum(axis=0)

    row_scale = lax.rsqrt(1.0 + arrived[:, F : F + 1])
    hidden = (features + arrived[:, :F]) * row_scale
    pre_act = jnp.dot(hidden, weight, precision=HIGHEST, preferred_element_type=jnp.float32)
    activated = jax.nn.softplus(pre_act)
    pulled = cotangent * jax.nn.sigmoid(pre_act) * row_scale

    pulled_block = to_all(pulled.astype(jnp.bfloat16), XY, N_XY)
    contract = (((0,), (0,)), ((), ()))
    term_other = lax.dot_general(adjacency[:, half:], pulled_block, contract, preferred_element_type=jnp.float32)
    from_other = to_other_core(term_other)
    term = lax.dot_general(adjacency[:, :half], pulled_block, contract, preferred_element_type=jnp.float32)
    term = (term + from_other).astype(jnp.bfloat16)
    term = exchange(term, "zl").reshape(N_Z_LO, N_Z_HI * RPD, F).astype(jnp.float32).sum(axis=0)
    term = exchange(term.astype(jnp.bfloat16), "zh").reshape(N_Z_HI, RPD, F).astype(jnp.float32).sum(axis=0)
    grad_input = lax.dot_general(
        pulled + term, weight, (((1,), (1,)), ((), ())), precision=HIGHEST, preferred_element_type=jnp.float32
    )
    return (activated, grad_input)


def solution(mesh):
    inner = Mesh(mesh.devices.reshape(N_Z_HI, N_Z_LO, N_X_HI, N_X_LO, N_Y, N_CORE), AXES)
    row, rep = ("zh", "zl", "xh"), ("xl", "y", "c")
    in_specs = (
        P(row + rep, None),
        P(),
        P(row + rep, None),
        P(row, rep),
        P(None, row),
        P(None, rep),
    )
    out_specs = (P(row + rep, None), P(row + rep, None))
    return jax.shard_map(per_device, mesh=inner, in_specs=in_specs, out_specs=out_specs, check_vma=False)
```

```python
import jax
import jax.numpy as jnp
from jax import lax
from jax.experimental import pallas as pl
from jax.experimental.pallas import tpu as pltpu
from jax.sharding import Mesh, PartitionSpec as P

HIGH = lax.Precision.HIGH
hash_prime = 65521
N_Z_HI, N_Z_LO, N_X_HI, N_X_LO, N_Y, N_CORE = 4, 4, 2, 2, 4, 2
N_Z = N_Z_HI * N_Z_LO
N_XY = N_X_HI * N_X_LO * N_Y
N_REP = N_X_LO * N_Y * N_CORE
RPD = 64
F = 512
R = N_XY * RPD
COLS = N_CORE * N_Z * RPD
HALF = COLS // 2
BLOCK = N_Z_HI * RPD
DIGITS = 16
AXES = ("zh", "zl", "xh", "xl", "y", "c")
Z = ("zh", "zl")
XY = ("xh", "xl", "y")


def centred(value):
    return value - jnp.round(value * (1.0 / hash_prime)) * float(hash_prime)


def two_digits(value):
    high = jnp.floor((value + 128.0) * (1.0 / 256.0))
    return value - 256.0 * high, high


def stack_rows(rows, width):
    row_index = lax.broadcasted_iota(jnp.int32, (DIGITS, width), 0)
    stacked = jnp.zeros((DIGITS, width), jnp.float32)
    for k, row in enumerate(rows):
        stacked = jnp.where(row_index == k, row, stacked)
    return stacked.astype(jnp.bfloat16)


def row_digits(first_code, second_code):
    digits = []
    for code in (first_code, second_code):
        for value in (code, centred(code * 256.0)):
            low, high = two_digits(value)
            digits.extend((low, 256.0 * high))
    low, high = two_digits(centred(centred((first_code + second_code) * 128.0) * 128.0))
    return digits + [low, 256.0 * high]


def column_digits(first_code, second_code):
    digits = []
    for code in (first_code, second_code):
        low, high = two_digits(code - 16384.0)
        digits.extend((low, low, high, high))
    return digits + [jnp.ones_like(first_code)] * 2


def adjacency_kernel(threshold_ref, rows_ref, columns_ref, mask_ref, adjacency_ref, degree_ref, left_ref):
    rows = rows_ref[...].astype(jnp.float32)
    columns = columns_ref[...].astype(jnp.float32)
    left_ref[...] = stack_rows(row_digits(rows[:1], rows[1:]), R)
    right = stack_rows(column_digits(columns[:1], columns[1:]), HALF)
    groups = (N_Z, HALF)
    spread = lax.broadcasted_iota(jnp.int32, groups, 0) == lax.broadcasted_iota(jnp.int32, groups, 1) // RPD
    spread = jnp.where(spread, 1.0, 0.0).astype(jnp.bfloat16)
    mask = mask_ref[...].astype(jnp.float32).astype(jnp.bfloat16)
    limit = jnp.dot(mask, spread, preferred_element_type=jnp.float32) * threshold_ref[0].astype(jnp.float32)
    ones = jnp.ones((8, HALF), jnp.bfloat16)
    for pair in range(N_XY // 2):
        at = pl.ds(2 * RPD * pair, 2 * RPD)
        contract = (((0,), (0,)), ((), ()))
        value = lax.dot_general(left_ref[:, at], right, contract, preferred_element_type=jnp.float32)
        nearest = jnp.round(value * (1.0 / hash_prime))
        residue = value - nearest * float(hash_prime)
        kept = []
        for k in range(2):
            part = residue[k * RPD : (k + 1) * RPD]
            inside = jnp.logical_and(part >= 0.0, part < limit[2 * pair + k][None, :])
            kept.append(jnp.where(inside, 1.0, 0.0))
        low = jnp.concatenate(kept, axis=0).astype(jnp.bfloat16)
        adjacency_ref[at, :] = low
        contract = (((1,), (1,)), ((), ()))
        degree_ref[:, at] = lax.dot_general(ones, low, contract, preferred_element_type=jnp.float32)


def build_adjacency(threshold, rows, columns, mask):
    vmem = pl.BlockSpec(memory_space=pltpu.VMEM)
    return pl.pallas_call(
        adjacency_kernel,
        in_specs=[pl.BlockSpec(memory_space=pltpu.SMEM), vmem, vmem, vmem],
        out_specs=[vmem, vmem],
        out_shape=[
            jax.ShapeDtypeStruct((R, HALF), jnp.bfloat16),
            jax.ShapeDtypeStruct((8, R), jnp.float32),
        ],
        scratch_shapes=[pltpu.VMEM((DIGITS, R), jnp.bfloat16)],
        compiler_params=pltpu.CompilerParams(vmem_limit_bytes=32 * 1024 * 1024),
        cost_estimate=pl.CostEstimate(flops=2 * R * HALF * 16, bytes_accessed=2 * R * HALF, transcendentals=0),
    )(threshold, rows, columns, mask)


def to_other_core(values):
    return lax.ppermute(values, "c", [(0, 1), (1, 0)])


def along_z(values, step):
    return lax.ppermute(values, Z, [(z, (z + step) % N_Z) for z in range(N_Z)])


def exchange(values, axis):
    return lax.all_to_all(values, axis, 0, 0, tiled=True)


def to_all(values, axis, count):
    return exchange(jnp.broadcast_to(values[None], (count,) + values.shape).reshape(-1, values.shape[1]), axis)


def per_device(features, weight, cotangent, tile_mask, row_codes, col_codes):
    x_hi, z_lo, core = lax.axis_index("xh"), lax.axis_index("zl"), lax.axis_index("c")
    subset = (lax.axis_index("xl") * N_Y + lax.axis_index("y")) * N_CORE + core

    def by_class(values):
        twice = jnp.concatenate([values, values], axis=1)
        turned = lax.dynamic_slice_in_dim(twice, z_lo, N_Z_LO, 1)
        return jnp.concatenate([turned[:, :2], turned[:, 3:], turned[:, 2:3]], axis=1)

    own_rows = lax.dynamic_index_in_dim(row_codes.reshape(2, N_XY // 2, N_CORE, RPD), core, 2, False)
    own_columns = lax.dynamic_index_in_dim(col_codes.reshape(2, N_Z_HI, N_Z_LO, N_X_HI, RPD), x_hi, 3, False)
    own_columns = by_class(own_columns.transpose(0, 2, 1, 3))
    own_mask = by_class(tile_mask.reshape(N_XY // 2, N_Z_HI, N_Z_LO).transpose(0, 2, 1))
    sizes = (own_rows.size, own_columns.size, own_mask.size)
    small = jnp.concatenate([own_rows.reshape(-1), own_columns.reshape(-1), own_mask.reshape(-1)])
    small = lax.all_gather(small, ("xh", "c"), axis=0).reshape(N_X_HI, N_CORE, -1)
    small = jnp.where(core == 0, small, small[:, ::-1])
    rows, other_rows = (
        small[:, k, : sizes[0]].reshape(N_X_HI, 2, R // 2).transpose(1, 0, 2).reshape(2, R) for k in range(N_CORE)
    )
    columns = lax.dynamic_index_in_dim(small[:, :, sizes[0] : sizes[0] + sizes[1]], x_hi, 0, False)
    columns = columns.reshape(N_CORE, 2, HALF)
    mask = small[:, :, sizes[0] + sizes[1] :].reshape(N_X_HI, N_CORE, N_XY // 2, N_Z)
    mask = mask.transpose(1, 0, 2, 3).reshape(N_CORE, N_XY, N_Z)
    thresholds = [
        ((10 + 20 * p // (N_REP - 1)) * hash_prime // 1000).astype(jnp.int32).reshape(1) for p in (subset, subset ^ 1)
    ]

    block = to_all(features.astype(jnp.bfloat16), "zh", N_Z_HI)
    block, rows, other_rows, columns, mask = lax.optimization_barrier((block, rows, other_rows, columns, mask))
    up, down = along_z(block, -1), along_z(block, 1)
    far_low, far_high = along_z(block[: BLOCK // 2], -2), along_z(block[BLOCK // 2 :], 2)
    own, own_degree = build_adjacency(thresholds[0], rows, columns[0], mask[0])
    other, other_degree = build_adjacency(thresholds[1], rows, columns[1], mask[1])
    degree = (own_degree + other_degree)[0].reshape(N_XY, 1, RPD).astype(jnp.float16)
    degree = jnp.pad(degree, ((0, 0), (0, 7), (0, F - RPD)))
    gathered = jnp.concatenate([block, up, down, far_low, far_high], axis=0)
    gathered, own, other, degree = lax.optimization_barrier((gathered, own, other, degree))
    aggregate = jnp.dot(own, gathered, preferred_element_type=jnp.float32)
    aggregate, gathered = lax.optimization_barrier((aggregate, to_other_core(gathered)))
    aggregate += jnp.dot(other, gathered, preferred_element_type=jnp.float32)
    sent = jnp.concatenate([aggregate.astype(jnp.float16).reshape(N_XY, RPD, F), degree], axis=1)
    arrived = lax.all_to_all(sent, XY, 0, 0).astype(jnp.float32).sum(axis=0)
    degree = arrived[RPD, :RPD][:, None]
    aggregate = arrived[:RPD]

    row_scale = lax.rsqrt(1.0 + degree)
    hidden = (features + aggregate) * row_scale
    pre_act = jnp.dot(hidden, weight, precision=HIGH, preferred_element_type=jnp.float32)
    activated = jax.nn.softplus(pre_act)
    pulled = cotangent * jax.nn.sigmoid(pre_act) * row_scale

    pulled_block = to_all(pulled.astype(jnp.bfloat16), XY, N_XY)
    contract = (((0,), (0,)), ((), ()))
    cross, _ = build_adjacency(thresholds[0], other_rows, columns[0], mask[0])
    term = lax.dot_general(own, pulled_block, contract, preferred_element_type=jnp.float32)
    term, cross, pulled_block = lax.optimization_barrier((term, cross, to_other_core(pulled_block)))
    term += lax.dot_general(cross, pulled_block, contract, preferred_element_type=jnp.float32)
    low = term[BLOCK:].astype(jnp.bfloat16)
    up, down = along_z(low[:BLOCK], 1), along_z(low[BLOCK : 2 * BLOCK], -1)
    far_low = along_z(low[2 * BLOCK : 2 * BLOCK + BLOCK // 2], 2)
    far_high = along_z(low[2 * BLOCK + BLOCK // 2 :], -2)
    far = jnp.concatenate([far_low, far_high], axis=0)
    term = term[:BLOCK] + up.astype(jnp.float32) + down.astype(jnp.float32) + far.astype(jnp.float32)
    term = exchange(term.astype(jnp.bfloat16), "zh").reshape(N_Z_HI, RPD, F).astype(jnp.float32).sum(axis=0)
    grad_input = lax.dot_general(
        pulled + term, weight, (((1,), (1,)), ((), ())), precision=HIGH, preferred_element_type=jnp.float32
    )
    return (activated, grad_input)


def solution(mesh):
    inner = Mesh(mesh.devices.reshape(N_Z_HI, N_Z_LO, N_X_HI, N_X_LO, N_Y, N_CORE), AXES)
    row, rep = ("zh", "zl", "xh"), ("xl", "y", "c")
    in_specs = (
        P(row + rep, None),
        P(),
        P(row + rep, None),
        P(row, rep),
        P(None, row),
        P(None, rep),
    )
    out_specs = (P(row + rep, None), P(row + rep, None))
    return jax.shard_map(per_device, mesh=inner, in_specs=in_specs, out_specs=out_specs, check_vma=False)
```

```python
import functools

import jax
import jax.numpy as jnp
from jax import lax
from jax.experimental import pallas as pl
from jax.experimental.pallas import tpu as pltpu
from jax.sharding import Mesh, PartitionSpec as P

HIGH = lax.Precision.HIGH
hash_prime = 65521
N_Z_HI, N_Z_LO, N_X_HI, N_X_LO, N_Y, N_CORE = 4, 4, 2, 2, 4, 2
N_Z = N_Z_HI * N_Z_LO
N_XY = N_X_HI * N_X_LO * N_Y
N_REP = N_X_LO * N_Y * N_CORE
RPD = 64
F = 512
R = N_XY * RPD
COLS = N_CORE * N_Z * RPD
HALF = COLS // 2
BLOCK = N_Z_HI * RPD
DIGITS = 16
AXES = ("zh", "zl", "xh", "xl", "y", "c")
Z = ("zh", "zl")
XY = ("xh", "xl", "y")


def centred(value):
    return value - jnp.round(value * (1.0 / hash_prime)) * float(hash_prime)


def two_digits(value):
    high = jnp.floor((value + 128.0) * (1.0 / 256.0))
    return value - 256.0 * high, high


def stack_rows(rows, width):
    row_index = lax.broadcasted_iota(jnp.int32, (DIGITS, width), 0)
    stacked = jnp.zeros((DIGITS, width), jnp.float32)
    for k, row in enumerate(rows):
        stacked = jnp.where(row_index == k, row, stacked)
    return stacked.astype(jnp.bfloat16)


def row_digits(first_code, second_code):
    digits = []
    for code in (first_code, second_code):
        for value in (code, centred(code * 256.0)):
            low, high = two_digits(value)
            digits.extend((low, 256.0 * high))
    low, high = two_digits(centred(centred((first_code + second_code) * 128.0) * 128.0))
    return digits + [low, 256.0 * high]


def column_digits(first_code, second_code):
    digits = []
    for code in (first_code, second_code):
        low, high = two_digits(code - 16384.0)
        digits.extend((low, low, high, high))
    return digits + [jnp.ones_like(first_code)] * 2


def halves(first, second, upper):
    lane = lax.broadcasted_iota(jnp.int32, first.shape, 1)
    lower_halves = jnp.where(lane < RPD, first, pltpu.roll(second, RPD, 1))
    upper_halves = jnp.where(lane < RPD, pltpu.roll(first, RPD, 1), second)
    return jnp.where(upper == 1, upper_halves, lower_halves)


def class_of(place, z_lo):
    return (z_lo + place + jnp.where(place == 2, 1, 0) - jnp.where(place == 3, 1, 0)) & (N_Z_LO - 1)


def adjacency_kernel(crossed, place_ref, codes_ref, *outs):
    own_ref, *others, picked_ref, left_ref = outs
    core, x_hi, z_lo = place_ref[0], place_ref[1], place_ref[2]

    for x in range(N_X_HI):
        for t in range(R // N_X_HI // 128):
            pieces = [codes_ref[N_CORE * x, :2, pl.ds(256 * t + 128 * k, 128)] for k in range(2)]
            picked_ref[:, pl.ds(R // N_X_HI * x + 128 * t, 128)] = halves(*pieces, core ^ 1 if crossed else core)
    rows = picked_ref[...].astype(jnp.float32)
    left_ref[...] = stack_rows(row_digits(rows[:1], rows[1:]), R)

    groups = (N_Z, HALF)
    column = lax.broadcasted_iota(jnp.int32, groups, 1)
    tile = ((column // RPD) & (N_Z_HI - 1)) * N_Z_LO + class_of(column // BLOCK, z_lo)
    spread = jnp.where(lax.broadcasted_iota(jnp.int32, groups, 0) == tile, 1.0, 0.0).astype(jnp.bfloat16)
    ones = jnp.ones((8, HALF), jnp.bfloat16)
    lane = lax.broadcasted_iota(jnp.int32, (8, 128), 1)
    for side in range(1 if crossed else 2):
        for place in range(N_Z_LO):
            for h in range(N_Z_HI // 2):
                pieces = []
                for k in range(2):
                    at = R + ((2 * h + k) * N_Z_LO + class_of(jnp.int32(place), z_lo)) * 128
                    pieces.append(codes_ref[core ^ side, :2, pl.ds(pl.multiple_of(at, 128), 128)])
                picked_ref[:, pl.ds(BLOCK * place + 128 * h, 128)] = halves(*pieces, x_hi)
        columns = picked_ref[...].astype(jnp.float32)
        right = stack_rows(column_digits(columns[:1], columns[1:]), HALF)
        masks = [codes_ref[N_CORE * x + (core ^ side), :, R + COLS : R + COLS + N_Z] for x in range(N_X_HI)]
        mask = jnp.concatenate(masks, axis=0).astype(jnp.float32).astype(jnp.bfloat16)
        limit = jnp.dot(mask, spread, preferred_element_type=jnp.float32) * place_ref[3 + side].astype(jnp.float32)
        for pair in range(N_XY // 2):
            at = pl.ds(2 * RPD * pair, 2 * RPD)
            contract = (((0,), (0,)), ((), ()))
            value = lax.dot_general(left_ref[:, at], right, contract, preferred_element_type=jnp.float32)
            nearest = jnp.round(value * (1.0 / hash_prime))
            residue = value - nearest * float(hash_prime)
            kept = []
            for k in range(2):
                part = residue[k * RPD : (k + 1) * RPD]
                inside = jnp.logical_and(part >= 0.0, part < limit[2 * pair + k][None, :])
                kept.append(jnp.where(inside, 1.0, 0.0))
            low = jnp.concatenate(kept, axis=0).astype(jnp.bfloat16)
            if crossed:
                own_ref[at, :] = low
                continue
            other_ref, degree_ref = others
            contract = (((1,), (1,)), ((), ()))
            count = lax.dot_general(ones, low, contract, preferred_element_type=jnp.float32)
            if side == 0:
                own_ref[at, :] = low
                degree_ref[2 * pair : 2 * pair + 2] = jnp.zeros((2, 8, 128), jnp.float32)
            else:
                other_ref[at, :] = low
            for k in range(2):
                part = pltpu.roll(count, RPD, 1) if k else count
                degree_ref[2 * pair + k] += jnp.where(lane < RPD, part, 0.0)


def build_adjacency(crossed, place, codes):
    vmem = pl.BlockSpec(memory_space=pltpu.VMEM)
    block = jax.ShapeDtypeStruct((R, HALF), jnp.bfloat16)
    outs = [block] if crossed else [block, block, jax.ShapeDtypeStruct((N_XY, 8, 128), jnp.float32)]
    return pl.pallas_call(
        functools.partial(adjacency_kernel, crossed),
        in_specs=[pl.BlockSpec(memory_space=pltpu.SMEM), vmem],
        out_specs=[vmem] * len(outs),
        out_shape=outs,
        scratch_shapes=[pltpu.VMEM((2, R), jnp.int32), pltpu.VMEM((DIGITS, R), jnp.bfloat16)],
        compiler_params=pltpu.CompilerParams(vmem_limit_bytes=6 * 1024 * 1024),
        cost_estimate=pl.CostEstimate(
            flops=2 * R * HALF * 16 * len(outs), bytes_accessed=2 * R * HALF * len(outs), transcendentals=0
        ),
    )(place, codes)


def prepare_kernel(features_ref, rows_ref, columns_ref, mask_ref, low_ref, codes_ref, values_ref, *scratch):
    *held, sems = scratch
    copies = [
        pltpu.make_async_copy(source, target, sems.at[k])
        for k, (source, target) in enumerate(zip((features_ref, rows_ref, columns_ref, mask_ref), (values_ref, *held)))
    ]
    for copy in copies:
        copy.start()
    codes_ref[...] = jnp.zeros_like(codes_ref)
    for copy in copies:
        copy.wait()
    rows, columns, mask = held
    for k in range(N_X_HI * N_CORE):
        codes_ref[k, :2, :R] = rows[...]
        codes_ref[k, :2, R : R + COLS] = columns[...]
        codes_ref[k, :, R + COLS : R + COLS + N_Z] = mask[...]
    low_ref[...] = values_ref[...].astype(jnp.bfloat16)


def prepare(features, row_codes, col_codes, tile_mask):
    vmem = pl.BlockSpec(memory_space=pltpu.VMEM)
    arrays = (features, row_codes, col_codes, tile_mask)
    return pl.pallas_call(
        prepare_kernel,
        in_specs=[pl.BlockSpec(memory_space=pl.ANY)] * 4,
        out_specs=[vmem, vmem],
        out_shape=[
            jax.ShapeDtypeStruct(features.shape, jnp.bfloat16),
            jax.ShapeDtypeStruct((N_X_HI * N_CORE, 8, R + COLS + 128), jnp.int32),
        ],
        scratch_shapes=[pltpu.VMEM(array.shape, array.dtype) for array in arrays] + [pltpu.SemaphoreType.DMA((4,))],
        compiler_params=pltpu.CompilerParams(vmem_limit_bytes=56 * 1024 * 1024),
    )(*arrays)


def multiply(left, right):
    return jnp.dot(left, right, preferred_element_type=jnp.float32)


def multiply_transposed(left, right):
    return lax.dot_general(left, right, (((0,), (0,)), ((), ())), preferred_element_type=jnp.float32)


def to_other_core(values):
    return lax.ppermute(values, "c", [(0, 1), (1, 0)])


def along_z(values, step):
    return lax.ppermute(values, Z, [(z, (z + step) % N_Z) for z in range(N_Z)])


def exchange(values, axis):
    return lax.all_to_all(values, axis, 0, 0, tiled=True)


def to_all(values, axis, count):
    return exchange(jnp.broadcast_to(values[None], (count,) + values.shape).reshape(-1, values.shape[1]), axis)


def per_device(features, weight, cotangent, tile_mask, row_codes, col_codes):
    x_hi, z_lo, core = lax.axis_index("xh"), lax.axis_index("zl"), lax.axis_index("c")
    subset = (lax.axis_index("xl") * N_Y + lax.axis_index("y")) * N_CORE + core

    thresholds = [(10 + 20 * p // (N_REP - 1)) * hash_prime // 1000 for p in (subset, subset ^ 1)]
    place = jnp.stack([core, x_hi, z_lo, *thresholds]).astype(jnp.int32)

    low, codes = prepare(features, row_codes, col_codes, tile_mask)
    codes = lax.all_to_all(codes, ("xh", "c"), 0, 0, tiled=True)
    block = lax.all_gather(low, "zh", axis=0, tiled=True)
    up, down = along_z(block, -1), along_z(block, 1)
    far = along_z(up, -1)
    own, other, degree = build_adjacency(False, place, codes)
    degree = jnp.pad(degree, ((0, 0), (0, 0), (0, F - 128))).astype(jnp.float16)
    gathered = jnp.concatenate([block, up, down, far], axis=0)
    gathered, own, other, degree = lax.optimization_barrier((gathered, own, other, degree))
    aggregate = multiply(own, gathered)
    aggregate, gathered = lax.optimization_barrier((aggregate, to_other_core(gathered)))
    aggregate += multiply(other, gathered)
    sent = jnp.concatenate([aggregate.astype(jnp.float16).reshape(N_XY, RPD, F), degree], axis=1)
    arrived = lax.all_to_all(sent, XY, 0, 0).astype(jnp.float32).sum(axis=0)
    degree = arrived[RPD, :RPD][:, None]
    aggregate = arrived[:RPD]

    row_scale = lax.rsqrt(1.0 + degree)
    hidden = (features + aggregate) * row_scale
    pre_act = jnp.dot(hidden, weight, precision=HIGH, preferred_element_type=jnp.float32)
    activated = jax.nn.softplus(pre_act)
    pulled = cotangent * jax.nn.sigmoid(pre_act) * row_scale

    pulled_block = to_all(pulled.astype(jnp.bfloat16), XY, N_XY)
    pulled_block, codes = lax.optimization_barrier((pulled_block, codes))
    (cross,) = build_adjacency(True, place, codes)
    far_term = multiply_transposed(own[:, 3 * BLOCK :], pulled_block)
    term = multiply_transposed(own[:, : 3 * BLOCK], pulled_block)
    far_term, term, pulled_other = lax.optimization_barrier((far_term, term, to_other_core(pulled_block)))
    far_term += multiply_transposed(cross[:, 3 * BLOCK :], pulled_other)
    passed = along_z(far_term.astype(jnp.bfloat16), 1)
    term += multiply_transposed(cross[:, : 3 * BLOCK], pulled_other)
    down = along_z(term[2 * BLOCK :].astype(jnp.bfloat16), -1)
    up = along_z((term[BLOCK : 2 * BLOCK] + passed.astype(jnp.float32)).astype(jnp.bfloat16), 1)
    term = term[:BLOCK] + up.astype(jnp.float32) + down.astype(jnp.float32)
    term = exchange(term.astype(jnp.bfloat16), "zh").reshape(N_Z_HI, RPD, F).astype(jnp.float32).sum(axis=0)
    grad_input = lax.dot_general(
        pulled + term, weight, (((1,), (1,)), ((), ())), precision=HIGH, preferred_element_type=jnp.float32
    )
    return (activated, grad_input)


def solution(mesh):
    inner = Mesh(mesh.devices.reshape(N_Z_HI, N_Z_LO, N_X_HI, N_X_LO, N_Y, N_CORE), AXES)
    row, rep = ("zh", "zl", "xh"), ("xl", "y", "c")
    in_specs = (
        P(row + rep, None),
        P(),
        P(row + rep, None),
        P(row, rep),
        P(None, row),
        P(None, rep),
    )
    out_specs = (P(row + rep, None), P(row + rep, None))
    return jax.shard_map(per_device, mesh=inner, in_specs=in_specs, out_specs=out_specs, check_vma=False)
```

```python
import jax
import jax.numpy as jnp
from jax import lax
from jax.experimental import pallas as pl
from jax.experimental.pallas import tpu as pltpu
from jax.sharding import Mesh, PartitionSpec as P

HIGH = lax.Precision.HIGH
hash_prime = 65521
N_Z_HI, N_Z_LO, N_X_HI, N_X_LO, N_Y, N_CORE = 4, 4, 2, 2, 4, 2
N_Z = N_Z_HI * N_Z_LO
N_XY = N_X_HI * N_X_LO * N_Y
N_REP = N_X_LO * N_Y * N_CORE
RPD = 64
F = 512
R = N_XY * RPD
COLS = N_CORE * N_Z * RPD
HALF = COLS // 2
BLOCK = N_Z_HI * RPD
DIGITS = 16
AXES = ("zh", "zl", "xh", "xl", "y", "c")
Z = ("zh", "zl")
XY = ("xh", "xl", "y")


def centred(value):
    return value - jnp.round(value * (1.0 / hash_prime)) * float(hash_prime)


def two_digits(value):
    high = jnp.floor((value + 128.0) * (1.0 / 256.0))
    return value - 256.0 * high, high


def stack_rows(rows, width):
    row_index = lax.broadcasted_iota(jnp.int32, (DIGITS, width), 0)
    stacked = jnp.zeros((DIGITS, width), jnp.float32)
    for k, row in enumerate(rows):
        stacked = jnp.where(row_index == k, row, stacked)
    return stacked.astype(jnp.bfloat16)


def row_digits(first_code, second_code):
    digits = []
    for code in (first_code, second_code):
        for value in (code, centred(code * 256.0)):
            low, high = two_digits(value)
            digits.extend((low, 256.0 * high))
    low, high = two_digits(centred(centred((first_code + second_code) * 128.0) * 128.0))
    return digits + [low, 256.0 * high]


def column_digits(first_code, second_code):
    digits = []
    for code in (first_code, second_code):
        low, high = two_digits(code - 16384.0)
        digits.extend((low, low, high, high))
    return digits + [jnp.ones_like(first_code)] * 2


def halves(first, second, upper):
    lane = lax.broadcasted_iota(jnp.int32, first.shape, 1)
    lower_halves = jnp.where(lane < RPD, first, pltpu.roll(second, RPD, 1))
    upper_halves = jnp.where(lane < RPD, pltpu.roll(first, RPD, 1), second)
    return jnp.where(upper == 1, upper_halves, lower_halves)


def class_of(place, z_lo):
    return (z_lo + place + jnp.where(place == 2, 1, 0) - jnp.where(place == 3, 1, 0)) & (N_Z_LO - 1)


def adjacency_kernel(place_ref, codes_ref, from_x_ref, *refs):
    own_ref, cross_ref, own_degree_ref, cross_degree_ref, picked_ref, left_ref = refs
    core, x_hi, z_lo = place_ref[0], place_ref[1], place_ref[2]

    for crossed in range(2):
        for x in range(N_X_HI):
            for t in range(R // N_X_HI // 128):
                pieces = []
                for k in range(2):
                    at = pl.ds(256 * t + 128 * k, 128)
                    pieces.append(jnp.where(x_hi == x, codes_ref[:2, at], from_x_ref[:2, at]))
                picked_ref[:, pl.ds(R // N_X_HI * x + 128 * t, 128)] = halves(*pieces, core ^ crossed)
        rows = picked_ref[...].astype(jnp.float32)
        left_ref[crossed] = stack_rows(row_digits(rows[:1], rows[1:]), R)

    groups = (N_Z, HALF)
    column = lax.broadcasted_iota(jnp.int32, groups, 1)
    tile = ((column // RPD) & (N_Z_HI - 1)) * N_Z_LO + class_of(column // BLOCK, z_lo)
    spread = jnp.where(lax.broadcasted_iota(jnp.int32, groups, 0) == tile, 1.0, 0.0).astype(jnp.bfloat16)
    ones = jnp.ones((8, HALF), jnp.bfloat16)
    lane = lax.broadcasted_iota(jnp.int32, (8, 128), 1)
    for place in range(N_Z_LO):
        for h in range(N_Z_HI // 2):
            pieces = []
            for k in range(2):
                at = R + ((2 * h + k) * N_Z_LO + class_of(jnp.int32(place), z_lo)) * 128
                pieces.append(codes_ref[:2, pl.ds(pl.multiple_of(at, 128), 128)])
            picked_ref[:, pl.ds(BLOCK * place + 128 * h, 128)] = halves(*pieces, x_hi)
    columns = picked_ref[...].astype(jnp.float32)
    right = stack_rows(column_digits(columns[:1], columns[1:]), HALF)
    masks = (codes_ref[:, R + COLS : R + COLS + N_Z], from_x_ref[:, R : R + N_Z])
    mask = jnp.concatenate([jnp.where(x_hi == x, *masks) for x in range(N_X_HI)], axis=0)
    mask = mask.astype(jnp.float32).astype(jnp.bfloat16)
    limit = jnp.dot(mask, spread, preferred_element_type=jnp.float32) * place_ref[3].astype(jnp.float32)

    for crossed, (block_ref, degree_ref) in enumerate(((own_ref, own_degree_ref), (cross_ref, cross_degree_ref))):
        for pair in range(N_XY // 2):
            at = pl.ds(2 * RPD * pair, 2 * RPD)
            contract = (((0,), (0,)), ((), ()))
            value = lax.dot_general(left_ref[crossed, :, at], right, contract, preferred_element_type=jnp.float32)
            nearest = jnp.round(value * (1.0 / hash_prime))
            residue = value - nearest * float(hash_prime)
            kept = []
            for k in range(2):
                part = residue[k * RPD : (k + 1) * RPD]
                inside = jnp.logical_and(part >= 0.0, part < limit[2 * pair + k][None, :])
                kept.append(jnp.where(inside, 1.0, 0.0))
            low = jnp.concatenate(kept, axis=0).astype(jnp.bfloat16)
            block_ref[at, :] = low
            contract = (((1,), (1,)), ((), ()))
            count = lax.dot_general(ones, low, contract, preferred_element_type=jnp.float32)
            for k in range(2):
                part = pltpu.roll(count, RPD, 1) if k else count
                degree_ref[2 * pair + k] = jnp.where(lane < RPD, part, 0.0)


def build_adjacency(place, codes, from_x):
    vmem = pl.BlockSpec(memory_space=pltpu.VMEM)
    block = jax.ShapeDtypeStruct((R, HALF), jnp.bfloat16)
    degree = jax.ShapeDtypeStruct((N_XY, 8, 128), jnp.float32)
    return pl.pallas_call(
        adjacency_kernel,
        in_specs=[pl.BlockSpec(memory_space=pltpu.SMEM), vmem, vmem],
        out_specs=[vmem] * 4,
        out_shape=[block, block, degree, degree],
        scratch_shapes=[pltpu.VMEM((2, R), jnp.int32), pltpu.VMEM((2, DIGITS, R), jnp.bfloat16)],
        compiler_params=pltpu.CompilerParams(vmem_limit_bytes=6 * 1024 * 1024),
        cost_estimate=pl.CostEstimate(flops=4 * R * HALF * 16, bytes_accessed=4 * R * HALF, transcendentals=0),
    )(place, codes, from_x)


def prepare_kernel(features_ref, rows_ref, columns_ref, mask_ref, low_ref, codes_ref, shared_ref, *scratch):
    values_ref, *held, sems = scratch
    copies = [
        pltpu.make_async_copy(source, target, sems.at[k])
        for k, (source, target) in enumerate(zip((features_ref, rows_ref, columns_ref, mask_ref), (values_ref, *held)))
    ]
    for copy in copies:
        copy.start()
    codes_ref[...] = jnp.zeros_like(codes_ref)
    shared_ref[...] = jnp.zeros_like(shared_ref)
    for copy in copies:
        copy.wait()
    rows, columns, mask = held
    codes_ref[:2, :R] = rows[...]
    codes_ref[:2, R : R + COLS] = columns[...]
    codes_ref[:, R + COLS : R + COLS + N_Z] = mask[...]
    shared_ref[:2, :R] = rows[...]
    shared_ref[:, R : R + N_Z] = mask[...]
    low_ref[...] = values_ref[...].astype(jnp.bfloat16)


def prepare(features, row_codes, col_codes, tile_mask):
    vmem = pl.BlockSpec(memory_space=pltpu.VMEM)
    arrays = (features, row_codes, col_codes, tile_mask)
    return pl.pallas_call(
        prepare_kernel,
        in_specs=[pl.BlockSpec(memory_space=pl.ANY)] * 4,
        out_specs=[vmem, vmem, vmem],
        out_shape=[
            jax.ShapeDtypeStruct(features.shape, jnp.bfloat16),
            jax.ShapeDtypeStruct((8, R + COLS + 128), jnp.int32),
            jax.ShapeDtypeStruct((8, R + 128), jnp.int32),
        ],
        scratch_shapes=[pltpu.VMEM(array.shape, array.dtype) for array in arrays] + [pltpu.SemaphoreType.DMA((4,))],
        compiler_params=pltpu.CompilerParams(vmem_limit_bytes=56 * 1024 * 1024),
    )(*arrays)


def multiply(left, right):
    return jnp.dot(left, right, preferred_element_type=jnp.float32)


def multiply_transposed(left, right):
    return lax.dot_general(left, right, (((0,), (0,)), ((), ())), preferred_element_type=jnp.float32)


def to_other_core(values):
    return lax.ppermute(values, "c", [(0, 1), (1, 0)])


def along_z(values, step):
    return lax.ppermute(values, Z, [(z, (z + step) % N_Z) for z in range(N_Z)])


def exchange(values, axis):
    return lax.all_to_all(values, axis, 0, 0, tiled=True)


def to_all(values, axis, count):
    return exchange(jnp.broadcast_to(values[None], (count,) + values.shape).reshape(-1, values.shape[1]), axis)


def per_device(features, weight, cotangent, tile_mask, row_codes, col_codes):
    x_hi, z_lo, core = lax.axis_index("xh"), lax.axis_index("zl"), lax.axis_index("c")
    subset = (lax.axis_index("xl") * N_Y + lax.axis_index("y")) * N_CORE + core

    threshold = (10 + 20 * subset // (N_REP - 1)) * hash_prime // 1000
    place = jnp.stack([core, x_hi, z_lo, threshold]).astype(jnp.int32)

    low, codes, shared = prepare(features, row_codes, col_codes, tile_mask)
    from_x = lax.ppermute(shared, "xh", [(0, 1), (1, 0)])
    block = lax.all_gather(low, "zh", axis=0, tiled=True)
    up, down = along_z(block, -1), along_z(block, 1)
    up, from_x = lax.optimization_barrier((up, from_x))
    far = along_z(up, -1)
    own, cross, own_degree, cross_degree = build_adjacency(place, codes, from_x)
    gathered = jnp.concatenate([block, up, down, far], axis=0)
    gathered, own, cross, own_degree, cross_degree = lax.optimization_barrier(
        (gathered, own, cross, own_degree, cross_degree)
    )

    def with_degree(aggregate, degree):
        degree = jnp.pad(degree, ((0, 0), (0, 0), (0, F - 128)))
        return jnp.concatenate([aggregate.reshape(N_XY, RPD, F), degree], axis=1)

    crossing = to_other_core(with_degree(multiply(cross, gathered), cross_degree).astype(jnp.float16))
    aggregate, crossing = lax.optimization_barrier((multiply(own, gathered), crossing))
    sent = (with_degree(aggregate, own_degree) + crossing.astype(jnp.float32)).astype(jnp.float16)
    arrived = lax.all_to_all(sent, XY, 0, 0).astype(jnp.float32).sum(axis=0)
    degree = arrived[RPD, :RPD][:, None]
    aggregate = arrived[:RPD]

    row_scale = lax.rsqrt(1.0 + degree)
    hidden = (features + aggregate) * row_scale
    pre_act = jnp.dot(hidden, weight, precision=HIGH, preferred_element_type=jnp.float32)
    activated = jax.nn.softplus(pre_act)
    pulled = cotangent * jax.nn.sigmoid(pre_act) * row_scale

    pulled_block = to_all(pulled.astype(jnp.bfloat16), XY, N_XY)
    far_term = multiply_transposed(own[:, 3 * BLOCK :], pulled_block)
    term = multiply_transposed(own[:, : 3 * BLOCK], pulled_block)
    far_term, term, pulled_other = lax.optimization_barrier((far_term, term, to_other_core(pulled_block)))
    far_term += multiply_transposed(cross[:, 3 * BLOCK :], pulled_other)
    passed = along_z(far_term.astype(jnp.bfloat16), 1)
    term += multiply_transposed(cross[:, : 3 * BLOCK], pulled_other)
    down = along_z(term[2 * BLOCK :].astype(jnp.bfloat16), -1)
    up = along_z((term[BLOCK : 2 * BLOCK] + passed.astype(jnp.float32)).astype(jnp.bfloat16), 1)
    term = term[:BLOCK] + up.astype(jnp.float32) + down.astype(jnp.float32)
    term = exchange(term.astype(jnp.bfloat16), "zh").reshape(N_Z_HI, RPD, F).astype(jnp.float32).sum(axis=0)
    grad_input = lax.dot_general(
        pulled + term, weight, (((1,), (1,)), ((), ())), precision=HIGH, preferred_element_type=jnp.float32
    )
    return (activated, grad_input)


def solution(mesh):
    inner = Mesh(mesh.devices.reshape(N_Z_HI, N_Z_LO, N_X_HI, N_X_LO, N_Y, N_CORE), AXES)
    row, rep = ("zh", "zl", "xh"), ("xl", "y", "c")
    in_specs = (
        P(row + rep, None),
        P(),
        P(row + rep, None),
        P(row, rep),
        P(None, row),
        P(None, rep),
    )
    out_specs = (P(row + rep, None), P(row + rep, None))
    return jax.shard_map(per_device, mesh=inner, in_specs=in_specs, out_specs=out_specs, check_vma=False)
```

```python
import jax
import jax.numpy as jnp
from jax import lax
from jax.experimental import pallas as pl
from jax.experimental.pallas import tpu as pltpu
from jax.sharding import Mesh, PartitionSpec as P

HIGH = lax.Precision.HIGH
hash_prime = 65521
N_Z_HI, N_Z_LO, N_X_HI, N_X_LO, N_Y, N_CORE = 4, 4, 2, 2, 4, 2
N_Z = N_Z_HI * N_Z_LO
N_XY = N_X_HI * N_X_LO * N_Y
N_REP = N_X_LO * N_Y * N_CORE
RPD = 64
F = 512
R = N_XY * RPD
COLS = N_CORE * N_Z * RPD
HALF = COLS // 2
BLOCK = N_Z_HI * RPD
DIGITS = 16
AXES = ("zh", "zl", "xh", "xl", "y", "c")
Z = ("zh", "zl")
XY = ("xh", "xl", "y")


def centred(value):
    return value - jnp.round(value * (1.0 / hash_prime)) * float(hash_prime)


def two_digits(value):
    high = jnp.floor((value + 128.0) * (1.0 / 256.0))
    return value - 256.0 * high, high


def stack_rows(rows, width):
    row_index = lax.broadcasted_iota(jnp.int32, (DIGITS, width), 0)
    stacked = jnp.zeros((DIGITS, width), jnp.float32)
    for k, row in enumerate(rows):
        stacked = jnp.where(row_index == k, row, stacked)
    return stacked.astype(jnp.bfloat16)


def row_digits(first_code, second_code):
    digits = []
    for code in (first_code, second_code):
        for value in (code, centred(code * 256.0)):
            low, high = two_digits(value)
            digits.extend((low, 256.0 * high))
    low, high = two_digits(centred(centred((first_code + second_code) * 128.0) * 128.0))
    return digits + [low, 256.0 * high]


def column_digits(first_code, second_code):
    digits = []
    for code in (first_code, second_code):
        low, high = two_digits(code - 16384.0)
        digits.extend((low, low, high, high))
    return digits + [jnp.ones_like(first_code)] * 2


def halves(first, second, upper):
    lane = lax.broadcasted_iota(jnp.int32, first.shape, 1)
    lower_halves = jnp.where(lane < RPD, first, pltpu.roll(second, RPD, 1))
    upper_halves = jnp.where(lane < RPD, pltpu.roll(first, RPD, 1), second)
    return jnp.where(upper == 1, upper_halves, lower_halves)


def class_of(place, z_lo):
    return (z_lo + place + jnp.where(place == 2, 1, 0) - jnp.where(place == 3, 1, 0)) & (N_Z_LO - 1)


def adjacency_kernel(place_ref, codes_ref, from_x_ref, *refs):
    own_ref, cross_ref, own_degree_ref, cross_degree_ref, picked_ref, left_ref = refs
    core, x_hi, z_lo = place_ref[0], place_ref[1], place_ref[2]

    for crossed in range(2):
        for x in range(N_X_HI):
            for t in range(R // N_X_HI // 128):
                pieces = []
                for k in range(2):
                    at = pl.ds(256 * t + 128 * k, 128)
                    pieces.append(jnp.where(x_hi == x, codes_ref[:2, at], from_x_ref[:2, at]))
                picked_ref[:, pl.ds(R // N_X_HI * x + 128 * t, 128)] = halves(*pieces, core ^ crossed)
        rows = picked_ref[...].astype(jnp.float32)
        left_ref[crossed] = stack_rows(row_digits(rows[:1], rows[1:]), R)

    groups = (N_Z, HALF)
    column = lax.broadcasted_iota(jnp.int32, groups, 1)
    tile = ((column // RPD) & (N_Z_HI - 1)) * N_Z_LO + class_of(column // BLOCK, z_lo)
    spread = jnp.where(lax.broadcasted_iota(jnp.int32, groups, 0) == tile, 1.0, 0.0).astype(jnp.bfloat16)
    ones = jnp.ones((8, HALF), jnp.bfloat16)
    lane = lax.broadcasted_iota(jnp.int32, (8, 128), 1)
    for place in range(N_Z_LO):
        for h in range(N_Z_HI // 2):
            pieces = []
            for k in range(2):
                at = R + ((2 * h + k) * N_Z_LO + class_of(jnp.int32(place), z_lo)) * 128
                pieces.append(codes_ref[:2, pl.ds(pl.multiple_of(at, 128), 128)])
            picked_ref[:, pl.ds(BLOCK * place + 128 * h, 128)] = halves(*pieces, x_hi)
    columns = picked_ref[...].astype(jnp.float32)
    right = stack_rows(column_digits(columns[:1], columns[1:]), HALF)
    masks = (codes_ref[:, R + COLS : R + COLS + N_Z], from_x_ref[:, R : R + N_Z])
    mask = jnp.concatenate([jnp.where(x_hi == x, *masks) for x in range(N_X_HI)], axis=0)
    mask = mask.astype(jnp.float32).astype(jnp.bfloat16)
    limit = jnp.dot(mask, spread, preferred_element_type=jnp.float32) * place_ref[3].astype(jnp.float32)

    for crossed, (block_ref, degree_ref) in enumerate(((own_ref, own_degree_ref), (cross_ref, cross_degree_ref))):
        for pair in range(N_XY // 2):
            at = pl.ds(2 * RPD * pair, 2 * RPD)
            contract = (((0,), (0,)), ((), ()))
            value = lax.dot_general(left_ref[crossed, :, at], right, contract, preferred_element_type=jnp.float32)
            nearest = jnp.round(value * (1.0 / hash_prime))
            residue = value - nearest * float(hash_prime)
            kept = []
            for k in range(2):
                part = residue[k * RPD : (k + 1) * RPD]
                inside = jnp.logical_and(part >= 0.0, part < limit[2 * pair + k][None, :])
                kept.append(jnp.where(inside, 1.0, 0.0))
            low = jnp.concatenate(kept, axis=0).astype(jnp.bfloat16)
            block_ref[at, :] = low
            contract = (((1,), (1,)), ((), ()))
            count = lax.dot_general(ones, low, contract, preferred_element_type=jnp.float32)
            for k in range(2):
                part = pltpu.roll(count, RPD, 1) if k else count
                degree_ref[2 * pair + k] = jnp.where(lane < RPD, part, 0.0)


def build_adjacency(place, codes, from_x):
    vmem = pl.BlockSpec(memory_space=pltpu.VMEM)
    block = jax.ShapeDtypeStruct((R, HALF), jnp.bfloat16)
    degree = jax.ShapeDtypeStruct((N_XY, 8, 128), jnp.float32)
    return pl.pallas_call(
        adjacency_kernel,
        in_specs=[pl.BlockSpec(memory_space=pltpu.SMEM), vmem, vmem],
        out_specs=[vmem] * 4,
        out_shape=[block, block, degree, degree],
        scratch_shapes=[pltpu.VMEM((2, R), jnp.int32), pltpu.VMEM((2, DIGITS, R), jnp.bfloat16)],
        compiler_params=pltpu.CompilerParams(vmem_limit_bytes=6 * 1024 * 1024),
        cost_estimate=pl.CostEstimate(flops=4 * R * HALF * 16, bytes_accessed=4 * R * HALF, transcendentals=0),
    )(place, codes, from_x)


def prepare_kernel(features_ref, rows_ref, columns_ref, mask_ref, low_ref, codes_ref, shared_ref, *scratch):
    values_ref, *held, sems = scratch
    copies = [
        pltpu.make_async_copy(source, target, sems.at[k])
        for k, (source, target) in enumerate(zip((features_ref, rows_ref, columns_ref, mask_ref), (values_ref, *held)))
    ]
    for copy in copies:
        copy.start()
    codes_ref[...] = jnp.zeros_like(codes_ref)
    shared_ref[...] = jnp.zeros_like(shared_ref)
    for copy in copies:
        copy.wait()
    rows, columns, mask = held
    codes_ref[:2, :R] = rows[...]
    codes_ref[:2, R : R + COLS] = columns[...]
    codes_ref[:, R + COLS : R + COLS + N_Z] = mask[...]
    shared_ref[:2, :R] = rows[...]
    shared_ref[:, R : R + N_Z] = mask[...]
    low_ref[...] = values_ref[...].astype(jnp.bfloat16)


def prepare(features, row_codes, col_codes, tile_mask):
    vmem = pl.BlockSpec(memory_space=pltpu.VMEM)
    arrays = (features, row_codes, col_codes, tile_mask)
    return pl.pallas_call(
        prepare_kernel,
        in_specs=[pl.BlockSpec(memory_space=pl.ANY)] * 4,
        out_specs=[vmem, vmem, vmem],
        out_shape=[
            jax.ShapeDtypeStruct(features.shape, jnp.bfloat16),
            jax.ShapeDtypeStruct((8, R + COLS + 128), jnp.int32),
            jax.ShapeDtypeStruct((8, R + 128), jnp.int32),
        ],
        scratch_shapes=[pltpu.VMEM(array.shape, array.dtype) for array in arrays] + [pltpu.SemaphoreType.DMA((4,))],
        compiler_params=pltpu.CompilerParams(vmem_limit_bytes=56 * 1024 * 1024),
    )(*arrays)


def class_sums_kernel(z_hi_ref, term_ref, up_ref, down_ref, *sum_refs):
    for step, sum_ref in enumerate(sum_refs):
        start = ((z_hi_ref[0] + step) & (N_Z_HI - 1)) * RPD
        at = pl.ds(pl.multiple_of(start, RPD), RPD)
        total = term_ref[at, :] + up_ref[at, :].astype(jnp.float32) + down_ref[at, :].astype(jnp.float32)
        sum_ref[...] = total.astype(sum_ref.dtype)


def class_sums(z_hi, term, up, down):
    vmem = pl.BlockSpec(memory_space=pltpu.VMEM)
    kinds = (jnp.float32, jnp.float32, jnp.bfloat16, jnp.bfloat16)
    return pl.pallas_call(
        class_sums_kernel,
        in_specs=[pl.BlockSpec(memory_space=pltpu.SMEM), vmem, vmem, vmem],
        out_specs=[vmem] * N_Z_HI,
        out_shape=[jax.ShapeDtypeStruct((RPD, F), kind) for kind in kinds],
        compiler_params=pltpu.CompilerParams(vmem_limit_bytes=4 * 1024 * 1024),
    )(z_hi.reshape(1).astype(jnp.int32), term, up, down)


def multiply(left, right):
    return jnp.dot(left, right, preferred_element_type=jnp.float32)


def multiply_transposed(left, right):
    return lax.dot_general(left, right, (((0,), (0,)), ((), ())), preferred_element_type=jnp.float32)


def to_other_core(values):
    return lax.ppermute(values, "c", [(0, 1), (1, 0)])


def along_z(values, step):
    return lax.ppermute(values, Z, [(z, (z + step) % N_Z) for z in range(N_Z)])


def exchange(values, axis):
    return lax.all_to_all(values, axis, 0, 0, tiled=True)


def to_all(values, axis, count):
    return exchange(jnp.broadcast_to(values[None], (count,) + values.shape).reshape(-1, values.shape[1]), axis)


def per_device(features, weight, cotangent, tile_mask, row_codes, col_codes):
    x_hi, z_lo, core = lax.axis_index("xh"), lax.axis_index("zl"), lax.axis_index("c")
    subset = (lax.axis_index("xl") * N_Y + lax.axis_index("y")) * N_CORE + core

    threshold = (10 + 20 * subset // (N_REP - 1)) * hash_prime // 1000
    place = jnp.stack([core, x_hi, z_lo, threshold]).astype(jnp.int32)

    low, codes, shared = prepare(features, row_codes, col_codes, tile_mask)
    from_x = lax.ppermute(shared, "xh", [(0, 1), (1, 0)])
    block = lax.all_gather(low, "zh", axis=0, tiled=True)
    up, down = along_z(block, -1), along_z(block, 1)
    up, from_x = lax.optimization_barrier((up, from_x))
    far = along_z(up, -1)
    own, cross, own_degree, cross_degree = build_adjacency(place, codes, from_x)
    gathered = jnp.concatenate([block, up, down, far], axis=0)
    gathered, own, cross, own_degree, cross_degree = lax.optimization_barrier(
        (gathered, own, cross, own_degree, cross_degree)
    )

    def with_degree(aggregate, degree):
        degree = jnp.pad(degree, ((0, 0), (0, 0), (0, F - 128)))
        return jnp.concatenate([aggregate.reshape(N_XY, RPD, F), degree], axis=1)

    crossing = to_other_core(with_degree(multiply(cross, gathered), cross_degree).astype(jnp.float16))
    aggregate, crossing = lax.optimization_barrier((multiply(own, gathered), crossing))
    sent = (with_degree(aggregate, own_degree) + crossing.astype(jnp.float32)).astype(jnp.float16)
    arrived = lax.all_to_all(sent, XY, 0, 0).astype(jnp.float32).sum(axis=0)
    degree = arrived[RPD, :RPD][:, None]
    aggregate = arrived[:RPD]

    row_scale = lax.rsqrt(1.0 + degree)
    hidden = (features + aggregate) * row_scale
    pre_act = jnp.dot(hidden, weight, precision=HIGH, preferred_element_type=jnp.float32)
    activated = jax.nn.softplus(pre_act)
    pulled = cotangent * jax.nn.sigmoid(pre_act) * row_scale

    pulled_block = to_all(pulled.astype(jnp.bfloat16), XY, N_XY)
    far_term = multiply_transposed(own[:, 3 * BLOCK :], pulled_block)
    term = multiply_transposed(own[:, : 3 * BLOCK], pulled_block)
    far_term, term, pulled_other = lax.optimization_barrier((far_term, term, to_other_core(pulled_block)))
    far_term += multiply_transposed(cross[:, 3 * BLOCK :], pulled_other)
    passed = along_z(far_term.astype(jnp.bfloat16), 1)
    term += multiply_transposed(cross[:, : 3 * BLOCK], pulled_other)
    down = along_z(term[2 * BLOCK :].astype(jnp.bfloat16), -1)
    up = along_z((term[BLOCK : 2 * BLOCK] + passed.astype(jnp.float32)).astype(jnp.bfloat16), 1)
    kept, ahead, opposite, behind = class_sums(lax.axis_index("zh"), term, up, down)
    passed = along_z(opposite, N_Z_LO)
    down = along_z(behind, -N_Z_LO)
    up = along_z((ahead + passed.astype(jnp.float32)).astype(jnp.bfloat16), N_Z_LO)
    term = kept + up.astype(jnp.float32) + down.astype(jnp.float32)
    grad_input = lax.dot_general(
        pulled + term, weight, (((1,), (1,)), ((), ())), precision=HIGH, preferred_element_type=jnp.float32
    )
    return (activated, grad_input)


def solution(mesh):
    inner = Mesh(mesh.devices.reshape(N_Z_HI, N_Z_LO, N_X_HI, N_X_LO, N_Y, N_CORE), AXES)
    row, rep = ("zh", "zl", "xh"), ("xl", "y", "c")
    in_specs = (
        P(row + rep, None),
        P(),
        P(row + rep, None),
        P(row, rep),
        P(None, row),
        P(None, rep),
    )
    out_specs = (P(row + rep, None), P(row + rep, None))
    return jax.shard_map(per_device, mesh=inner, in_specs=in_specs, out_specs=out_specs, check_vma=False)
```

```python
import jax
import jax.numpy as jnp
from jax import lax
from jax.experimental import pallas as pl
from jax.experimental.pallas import tpu as pltpu
from jax.sharding import Mesh, PartitionSpec as P

HIGH = lax.Precision.HIGH
hash_prime = 65521
N_Z_HI, N_Z_LO, N_X_HI, N_X_LO, N_Y, N_CORE = 4, 4, 2, 2, 4, 2
N_Z = N_Z_HI * N_Z_LO
N_XY = N_X_HI * N_X_LO * N_Y
N_REP = N_X_LO * N_Y * N_CORE
RPD = 64
F = 512
R = N_XY * RPD
COLS = N_CORE * N_Z * RPD
HALF = COLS // 2
BLOCK = N_Z_HI * RPD
DIGITS = 16
AXES = ("zh", "zl", "xh", "xl", "y", "c")
Z = ("zh", "zl")
XY = ("xh", "xl", "y")


def centred(value):
    return value - jnp.round(value * (1.0 / hash_prime)) * float(hash_prime)


def two_digits(value):
    high = jnp.floor((value + 128.0) * (1.0 / 256.0))
    return value - 256.0 * high, high


def stack_rows(rows, width):
    row_index = lax.broadcasted_iota(jnp.int32, (DIGITS, width), 0)
    stacked = jnp.zeros((DIGITS, width), jnp.float32)
    for k, row in enumerate(rows):
        stacked = jnp.where(row_index == k, row, stacked)
    return stacked.astype(jnp.bfloat16)


def row_digits(first_code, second_code):
    digits = []
    for code in (first_code, second_code):
        for value in (code, centred(code * 256.0)):
            low, high = two_digits(value)
            digits.extend((low, 256.0 * high))
    low, high = two_digits(centred(centred((first_code + second_code) * 128.0) * 128.0))
    return digits + [low, 256.0 * high]


def column_digits(first_code, second_code):
    digits = []
    for code in (first_code, second_code):
        low, high = two_digits(code - 16384.0)
        digits.extend((low, low, high, high))
    return digits + [jnp.ones_like(first_code)] * 2


def halves(first, second, upper):
    lane = lax.broadcasted_iota(jnp.int32, first.shape, 1)
    lower_halves = jnp.where(lane < RPD, first, pltpu.roll(second, RPD, 1))
    upper_halves = jnp.where(lane < RPD, pltpu.roll(first, RPD, 1), second)
    return jnp.where(upper == 1, upper_halves, lower_halves)


def class_of(place, z_lo):
    return (z_lo + place + jnp.where(place == 2, 1, 0) - jnp.where(place == 3, 1, 0)) & (N_Z_LO - 1)


def adjacency_kernel(place_ref, codes_ref, from_x_ref, *refs):
    own_ref, cross_ref, own_degree_ref, cross_degree_ref, picked_ref, left_ref = refs
    core, x_hi, z_lo = place_ref[0], place_ref[1], place_ref[2]

    for crossed in range(2):
        for x in range(N_X_HI):
            for t in range(R // N_X_HI // 128):
                pieces = []
                for k in range(2):
                    at = pl.ds(256 * t + 128 * k, 128)
                    pieces.append(jnp.where(x_hi == x, codes_ref[:2, at], from_x_ref[:2, at]))
                picked_ref[:, pl.ds(R // N_X_HI * x + 128 * t, 128)] = halves(*pieces, core ^ crossed)
        rows = picked_ref[...].astype(jnp.float32)
        left_ref[crossed] = stack_rows(row_digits(rows[:1], rows[1:]), R)

    groups = (N_Z, HALF)
    column = lax.broadcasted_iota(jnp.int32, groups, 1)
    tile = ((column // RPD) & (N_Z_HI - 1)) * N_Z_LO + class_of(column // BLOCK, z_lo)
    spread = jnp.where(lax.broadcasted_iota(jnp.int32, groups, 0) == tile, 1.0, 0.0).astype(jnp.bfloat16)
    ones = jnp.ones((8, HALF), jnp.bfloat16)
    lane = lax.broadcasted_iota(jnp.int32, (8, 128), 1)
    for place in range(N_Z_LO):
        for h in range(N_Z_HI // 2):
            pieces = []
            for k in range(2):
                at = R + ((2 * h + k) * N_Z_LO + class_of(jnp.int32(place), z_lo)) * 128
                pieces.append(codes_ref[:2, pl.ds(pl.multiple_of(at, 128), 128)])
            picked_ref[:, pl.ds(BLOCK * place + 128 * h, 128)] = halves(*pieces, x_hi)
    columns = picked_ref[...].astype(jnp.float32)
    right = stack_rows(column_digits(columns[:1], columns[1:]), HALF)
    masks = (codes_ref[:, R + COLS : R + COLS + N_Z], from_x_ref[:, R : R + N_Z])
    mask = jnp.concatenate([jnp.where(x_hi == x, *masks) for x in range(N_X_HI)], axis=0)
    mask = mask.astype(jnp.float32).astype(jnp.bfloat16)
    limit = jnp.dot(mask, spread, preferred_element_type=jnp.float32) * place_ref[3].astype(jnp.float32)

    for crossed, (block_ref, degree_ref) in enumerate(((own_ref, own_degree_ref), (cross_ref, cross_degree_ref))):
        for pair in range(N_XY // 2):
            at = pl.ds(2 * RPD * pair, 2 * RPD)
            contract = (((0,), (0,)), ((), ()))
            value = lax.dot_general(left_ref[crossed, :, at], right, contract, preferred_element_type=jnp.float32)
            nearest = jnp.round(value * (1.0 / hash_prime))
            residue = value - nearest * float(hash_prime)
            kept = []
            for k in range(2):
                part = residue[k * RPD : (k + 1) * RPD]
                inside = jnp.logical_and(part >= 0.0, part < limit[2 * pair + k][None, :])
                kept.append(jnp.where(inside, 1.0, 0.0))
            low = jnp.concatenate(kept, axis=0).astype(jnp.bfloat16)
            block_ref[at, :] = low
            contract = (((1,), (1,)), ((), ()))
            count = lax.dot_general(ones, low, contract, preferred_element_type=jnp.float32)
            for k in range(2):
                part = pltpu.roll(count, RPD, 1) if k else count
                degree_ref[2 * pair + k] = jnp.where(lane < RPD, part, 0.0)


def build_adjacency(place, codes, from_x):
    vmem = pl.BlockSpec(memory_space=pltpu.VMEM)
    block = jax.ShapeDtypeStruct((R, HALF), jnp.bfloat16)
    degree = jax.ShapeDtypeStruct((N_XY, 8, 128), jnp.float32)
    return pl.pallas_call(
        adjacency_kernel,
        in_specs=[pl.BlockSpec(memory_space=pltpu.SMEM), vmem, vmem],
        out_specs=[vmem] * 4,
        out_shape=[block, block, degree, degree],
        scratch_shapes=[pltpu.VMEM((2, R), jnp.int32), pltpu.VMEM((2, DIGITS, R), jnp.bfloat16)],
        compiler_params=pltpu.CompilerParams(vmem_limit_bytes=6 * 1024 * 1024),
        cost_estimate=pl.CostEstimate(flops=4 * R * HALF * 16, bytes_accessed=4 * R * HALF, transcendentals=0),
    )(place, codes, from_x)


def prepare_kernel(features_ref, rows_ref, columns_ref, mask_ref, low_ref, codes_ref, shared_ref, *scratch):
    values_ref, *held, sems = scratch
    copies = [
        pltpu.make_async_copy(source, target, sems.at[k])
        for k, (source, target) in enumerate(zip((features_ref, rows_ref, columns_ref, mask_ref), (values_ref, *held)))
    ]
    for copy in copies:
        copy.start()
    codes_ref[...] = jnp.zeros_like(codes_ref)
    shared_ref[...] = jnp.zeros_like(shared_ref)
    for copy in copies:
        copy.wait()
    rows, columns, mask = held
    codes_ref[:2, :R] = rows[...]
    codes_ref[:2, R : R + COLS] = columns[...]
    codes_ref[:, R + COLS : R + COLS + N_Z] = mask[...]
    shared_ref[:2, :R] = rows[...]
    shared_ref[:, R : R + N_Z] = mask[...]
    low_ref[...] = values_ref[...].astype(jnp.bfloat16)


def prepare(features, row_codes, col_codes, tile_mask):
    vmem = pl.BlockSpec(memory_space=pltpu.VMEM)
    arrays = (features, row_codes, col_codes, tile_mask)
    return pl.pallas_call(
        prepare_kernel,
        in_specs=[pl.BlockSpec(memory_space=pl.ANY)] * 4,
        out_specs=[vmem, vmem, vmem],
        out_shape=[
            jax.ShapeDtypeStruct(features.shape, jnp.bfloat16),
            jax.ShapeDtypeStruct((8, R + COLS + 128), jnp.int32),
            jax.ShapeDtypeStruct((8, R + 128), jnp.int32),
        ],
        scratch_shapes=[pltpu.VMEM(array.shape, array.dtype) for array in arrays] + [pltpu.SemaphoreType.DMA((4,))],
        compiler_params=pltpu.CompilerParams(vmem_limit_bytes=56 * 1024 * 1024),
    )(*arrays)


def class_sums_kernel(z_hi_ref, term_ref, up_ref, down_ref, *sum_refs):
    for step, sum_ref in enumerate(sum_refs):
        start = ((z_hi_ref[0] + step) & (N_Z_HI - 1)) * RPD
        at = pl.ds(pl.multiple_of(start, RPD), RPD)
        total = term_ref[at, :] + up_ref[at, :].astype(jnp.float32) + down_ref[at, :].astype(jnp.float32)
        sum_ref[...] = total.astype(sum_ref.dtype)


def class_sums(z_hi, term, up, down):
    vmem = pl.BlockSpec(memory_space=pltpu.VMEM)
    kinds = (jnp.float32, jnp.float32, jnp.bfloat16, jnp.bfloat16)
    return pl.pallas_call(
        class_sums_kernel,
        in_specs=[pl.BlockSpec(memory_space=pltpu.SMEM), vmem, vmem, vmem],
        out_specs=[vmem] * N_Z_HI,
        out_shape=[jax.ShapeDtypeStruct((RPD, F), kind) for kind in kinds],
        compiler_params=pltpu.CompilerParams(vmem_limit_bytes=4 * 1024 * 1024),
    )(z_hi.reshape(1).astype(jnp.int32), term, up, down)


def multiply(left, right):
    return jnp.dot(left, right, preferred_element_type=jnp.float32)


def multiply_transposed(left, right):
    return lax.dot_general(left, right, (((0,), (0,)), ((), ())), preferred_element_type=jnp.float32)


def to_other_core(values):
    return lax.ppermute(values, "c", [(0, 1), (1, 0)])


def along_z(values, step):
    return lax.ppermute(values, Z, [(z, (z + step) % N_Z) for z in range(N_Z)])


def exchange(values, axis):
    return lax.all_to_all(values, axis, 0, 0, tiled=True)


def to_all(values, axis, count):
    return exchange(jnp.broadcast_to(values[None], (count,) + values.shape).reshape(-1, values.shape[1]), axis)


def per_device(features, weight, cotangent, tile_mask, row_codes, col_codes):
    x_hi, z_lo, core = lax.axis_index("xh"), lax.axis_index("zl"), lax.axis_index("c")
    subset = (lax.axis_index("xl") * N_Y + lax.axis_index("y")) * N_CORE + core

    threshold = (10 + 20 * subset // (N_REP - 1)) * hash_prime // 1000
    place = jnp.stack([core, x_hi, z_lo, threshold]).astype(jnp.int32)

    low, codes, shared = prepare(features, row_codes, col_codes, tile_mask)
    from_x = lax.ppermute(shared, "xh", [(0, 1), (1, 0)])
    block = lax.all_gather(low, "zh", axis=0, tiled=True)
    up, down = along_z(block, -1), along_z(block, 1)
    up, from_x = lax.optimization_barrier((up, from_x))
    far = along_z(up, -1)
    own, cross, own_degree, cross_degree = build_adjacency(place, codes, from_x)
    gathered = jnp.concatenate([block, up, down, far], axis=0)
    gathered, own, cross, own_degree, cross_degree = lax.optimization_barrier(
        (gathered, own, cross, own_degree, cross_degree)
    )

    def with_degree(aggregate, degree):
        degree = jnp.pad(degree, ((0, 0), (0, 0), (0, F - 128)))
        return jnp.concatenate([aggregate.reshape(N_XY, RPD, F), degree], axis=1)

    crossing = to_other_core(with_degree(multiply(cross, gathered), cross_degree).astype(jnp.float16))
    aggregate, crossing = lax.optimization_barrier((multiply(own, gathered), crossing))
    sent = (with_degree(aggregate, own_degree) + crossing.astype(jnp.float32)).astype(jnp.float16)
    arrived = lax.all_to_all(sent, XY, 0, 0).astype(jnp.float32).sum(axis=0)
    degree = arrived[RPD, :RPD][:, None]
    aggregate = arrived[:RPD]

    row_scale = lax.rsqrt(1.0 + degree)
    hidden = (features + aggregate) * row_scale
    pre_act = jnp.dot(hidden, weight, precision=HIGH, preferred_element_type=jnp.float32)
    activated = jax.nn.softplus(pre_act)
    pulled = cotangent * jax.nn.sigmoid(pre_act) * row_scale

    pulled_block = to_all(pulled.astype(jnp.bfloat16), XY, N_XY)
    far_term = multiply_transposed(own[:, 3 * BLOCK :], pulled_block)
    term = multiply_transposed(own[:, : 3 * BLOCK], pulled_block)
    far_term, term, pulled_other = lax.optimization_barrier((far_term, term, to_other_core(pulled_block)))
    far_term += multiply_transposed(cross[:, 3 * BLOCK :], pulled_other)
    passed = along_z(far_term.astype(jnp.bfloat16), 1)
    term += multiply_transposed(cross[:, : 3 * BLOCK], pulled_other)
    down = along_z(term[2 * BLOCK :].astype(jnp.bfloat16), -1)
    up = along_z((term[BLOCK : 2 * BLOCK] + passed.astype(jnp.float32)).astype(jnp.bfloat16), 1)
    kept, ahead, opposite, behind = class_sums(lax.axis_index("zh"), term[:BLOCK], up, down)
    passed = along_z(opposite, N_Z_LO)
    down = along_z(behind, -N_Z_LO)
    up = along_z((ahead + passed.astype(jnp.float32)).astype(jnp.bfloat16), N_Z_LO)
    term = kept + up.astype(jnp.float32) + down.astype(jnp.float32)
    grad_input = lax.dot_general(
        pulled + term, weight, (((1,), (1,)), ((), ())), precision=HIGH, preferred_element_type=jnp.float32
    )
    return (activated, grad_input)


def solution(mesh):
    inner = Mesh(mesh.devices.reshape(N_Z_HI, N_Z_LO, N_X_HI, N_X_LO, N_Y, N_CORE), AXES)
    row, rep = ("zh", "zl", "xh"), ("xl", "y", "c")
    in_specs = (
        P(row + rep, None),
        P(),
        P(row + rep, None),
        P(row, rep),
        P(None, row),
        P(None, rep),
    )
    out_specs = (P(row + rep, None), P(row + rep, None))
    return jax.shard_map(per_device, mesh=inner, in_specs=in_specs, out_specs=out_specs, check_vma=False)
```

```python
import jax
import jax.numpy as jnp
from jax import lax
from jax.experimental import pallas as pl
from jax.experimental.pallas import tpu as pltpu
from jax.sharding import Mesh, PartitionSpec as P

HIGH = lax.Precision.HIGH
hash_prime = 65521
N_Z_HI, N_Z_LO, N_X_HI, N_X_LO, N_Y, N_CORE = 4, 4, 2, 2, 4, 2
N_Z = N_Z_HI * N_Z_LO
N_XY = N_X_HI * N_X_LO * N_Y
N_REP = N_X_LO * N_Y * N_CORE
RPD = 64
F = 512
R = N_XY * RPD
COLS = N_CORE * N_Z * RPD
HALF = COLS // 2
BLOCK = N_Z_HI * RPD
DIGITS = 16
AXES = ("zh", "zl", "xh", "xl", "y", "c")
Z = ("zh", "zl")
XY = ("xh", "xl", "y")


def centred(value):
    return value - jnp.round(value * (1.0 / hash_prime)) * float(hash_prime)


def two_digits(value):
    high = jnp.floor((value + 128.0) * (1.0 / 256.0))
    return value - 256.0 * high, high


def stack_rows(rows, width):
    row_index = lax.broadcasted_iota(jnp.int32, (DIGITS, width), 0)
    stacked = jnp.zeros((DIGITS, width), jnp.float32)
    for k, row in enumerate(rows):
        stacked = jnp.where(row_index == k, row, stacked)
    return stacked.astype(jnp.bfloat16)


def row_digits(first_code, second_code):
    digits = []
    for code in (first_code, second_code):
        for value in (code, centred(code * 256.0)):
            low, high = two_digits(value)
            digits.extend((low, 256.0 * high))
    low, high = two_digits(centred(centred((first_code + second_code) * 128.0) * 128.0))
    return digits + [low, 256.0 * high]


def column_digits(first_code, second_code):
    digits = []
    for code in (first_code, second_code):
        low, high = two_digits(code - 16384.0)
        digits.extend((low, low, high, high))
    return digits + [jnp.ones_like(first_code)] * 2


def halves(first, second, upper):
    lane = lax.broadcasted_iota(jnp.int32, first.shape, 1)
    lower_halves = jnp.where(lane < RPD, first, pltpu.roll(second, RPD, 1))
    upper_halves = jnp.where(lane < RPD, pltpu.roll(first, RPD, 1), second)
    return jnp.where(upper == 1, upper_halves, lower_halves)


def class_of(place, z_lo):
    return (z_lo + place + jnp.where(place == 2, 1, 0) - jnp.where(place == 3, 1, 0)) & (N_Z_LO - 1)


def adjacency_kernel(place_ref, codes_ref, from_x_ref, *refs):
    own_ref, cross_ref, own_degree_ref, cross_degree_ref, picked_ref, left_ref = refs
    core, x_hi, z_lo = place_ref[0], place_ref[1], place_ref[2]

    for crossed in range(2):
        for x in range(N_X_HI):
            for t in range(R // N_X_HI // 128):
                pieces = []
                for k in range(2):
                    at = pl.ds(256 * t + 128 * k, 128)
                    pieces.append(jnp.where(x_hi == x, codes_ref[:2, at], from_x_ref[:2, at].astype(jnp.float32)))
                picked_ref[:, pl.ds(R // N_X_HI * x + 128 * t, 128)] = halves(*pieces, core ^ crossed)
        rows = picked_ref[...]
        left_ref[crossed] = stack_rows(row_digits(rows[:1], rows[1:]), R)

    groups = (N_Z, HALF)
    column = lax.broadcasted_iota(jnp.int32, groups, 1)
    tile = ((column // RPD) & (N_Z_HI - 1)) * N_Z_LO + class_of(column // BLOCK, z_lo)
    spread = jnp.where(lax.broadcasted_iota(jnp.int32, groups, 0) == tile, 1.0, 0.0).astype(jnp.bfloat16)
    ones = jnp.ones((8, HALF), jnp.bfloat16)
    lane = lax.broadcasted_iota(jnp.int32, (8, 128), 1)
    for place in range(N_Z_LO):
        for h in range(N_Z_HI // 2):
            pieces = []
            for k in range(2):
                at = R + ((2 * h + k) * N_Z_LO + class_of(jnp.int32(place), z_lo)) * 128
                pieces.append(codes_ref[:2, pl.ds(pl.multiple_of(at, 128), 128)])
            picked_ref[:, pl.ds(BLOCK * place + 128 * h, 128)] = halves(*pieces, x_hi)
    columns = picked_ref[...]
    right = stack_rows(column_digits(columns[:1], columns[1:]), HALF)
    masks = (codes_ref[:, R + COLS : R + COLS + N_Z], from_x_ref[:, R : R + N_Z].astype(jnp.float32))
    mask = jnp.concatenate([jnp.where(x_hi == x, *masks) for x in range(N_X_HI)], axis=0)
    mask = mask.astype(jnp.bfloat16)
    limit = jnp.dot(mask, spread, preferred_element_type=jnp.float32) * place_ref[3].astype(jnp.float32)

    for crossed, (block_ref, degree_ref) in enumerate(((own_ref, own_degree_ref), (cross_ref, cross_degree_ref))):
        for pair in range(N_XY // 2):
            at = pl.ds(2 * RPD * pair, 2 * RPD)
            contract = (((0,), (0,)), ((), ()))
            value = lax.dot_general(left_ref[crossed, :, at], right, contract, preferred_element_type=jnp.float32)
            nearest = jnp.round(value * (1.0 / hash_prime))
            residue = value - nearest * float(hash_prime)
            kept = []
            for k in range(2):
                part = residue[k * RPD : (k + 1) * RPD]
                inside = jnp.logical_and(part >= 0.0, part < limit[2 * pair + k][None, :])
                kept.append(jnp.where(inside, 1.0, 0.0))
            low = jnp.concatenate(kept, axis=0).astype(jnp.bfloat16)
            block_ref[at, :] = low
            contract = (((1,), (1,)), ((), ()))
            count = lax.dot_general(ones, low, contract, preferred_element_type=jnp.float32)
            for k in range(2):
                part = pltpu.roll(count, RPD, 1) if k else count
                degree_ref[2 * pair + k] = jnp.where(lane < RPD, part, 0.0)


def build_adjacency(place, codes, from_x):
    vmem = pl.BlockSpec(memory_space=pltpu.VMEM)
    block = jax.ShapeDtypeStruct((R, HALF), jnp.bfloat16)
    degree = jax.ShapeDtypeStruct((N_XY, 8, 128), jnp.float32)
    return pl.pallas_call(
        adjacency_kernel,
        in_specs=[pl.BlockSpec(memory_space=pltpu.SMEM), vmem, vmem],
        out_specs=[vmem] * 4,
        out_shape=[block, block, degree, degree],
        scratch_shapes=[pltpu.VMEM((2, R), jnp.float32), pltpu.VMEM((2, DIGITS, R), jnp.bfloat16)],
        compiler_params=pltpu.CompilerParams(vmem_limit_bytes=6 * 1024 * 1024),
        cost_estimate=pl.CostEstimate(flops=4 * R * HALF * 16, bytes_accessed=4 * R * HALF, transcendentals=0),
    )(place, codes, from_x)


def prepare_kernel(features_ref, rows_ref, columns_ref, mask_ref, low_ref, codes_ref, shared_ref, *scratch):
    values_ref, *held, sems = scratch
    copies = [
        pltpu.make_async_copy(source, target, sems.at[k])
        for k, (source, target) in enumerate(zip((features_ref, rows_ref, columns_ref, mask_ref), (values_ref, *held)))
    ]
    for copy in copies:
        copy.start()
    codes_ref[...] = jnp.zeros_like(codes_ref)
    shared_ref[...] = jnp.zeros_like(shared_ref)
    for copy in copies:
        copy.wait()
    rows, columns, mask = held
    codes_ref[:2, :R] = rows[...]
    codes_ref[:2, R : R + COLS] = columns[...]
    codes_ref[:, R + COLS : R + COLS + N_Z] = mask[...]
    shared_ref[:2, :R] = rows[...]
    shared_ref[:, R : R + N_Z] = mask[...]
    low_ref[...] = values_ref[...].astype(jnp.bfloat16)


def prepare(features, row_codes, col_codes, tile_mask):
    vmem = pl.BlockSpec(memory_space=pltpu.VMEM)
    arrays = (features, row_codes, col_codes, tile_mask)
    return pl.pallas_call(
        prepare_kernel,
        in_specs=[pl.BlockSpec(memory_space=pl.ANY)] * 4,
        out_specs=[vmem, vmem, vmem],
        out_shape=[
            jax.ShapeDtypeStruct(features.shape, jnp.bfloat16),
            jax.ShapeDtypeStruct((8, R + COLS + 128), jnp.int32),
            jax.ShapeDtypeStruct((8, R + 128), jnp.int32),
        ],
        scratch_shapes=[pltpu.VMEM(array.shape, array.dtype) for array in arrays] + [pltpu.SemaphoreType.DMA((4,))],
        compiler_params=pltpu.CompilerParams(vmem_limit_bytes=56 * 1024 * 1024),
    )(*arrays)


def class_sums_kernel(z_hi_ref, term_ref, up_ref, down_ref, *sum_refs):
    for step, sum_ref in enumerate(sum_refs):
        start = ((z_hi_ref[0] + step) & (N_Z_HI - 1)) * RPD
        at = pl.ds(pl.multiple_of(start, RPD), RPD)
        total = term_ref[at, :] + up_ref[at, :].astype(jnp.float32) + down_ref[at, :].astype(jnp.float32)
        sum_ref[...] = total.astype(sum_ref.dtype)


def class_sums(z_hi, term, up, down):
    vmem = pl.BlockSpec(memory_space=pltpu.VMEM)
    kinds = (jnp.float32, jnp.float32, jnp.bfloat16, jnp.bfloat16)
    return pl.pallas_call(
        class_sums_kernel,
        in_specs=[pl.BlockSpec(memory_space=pltpu.SMEM), vmem, vmem, vmem],
        out_specs=[vmem] * N_Z_HI,
        out_shape=[jax.ShapeDtypeStruct((RPD, F), kind) for kind in kinds],
        compiler_params=pltpu.CompilerParams(vmem_limit_bytes=4 * 1024 * 1024),
    )(z_hi.reshape(1).astype(jnp.int32), term, up, down)


def multiply(left, right):
    return jnp.dot(left, right, preferred_element_type=jnp.float32)


def multiply_transposed(left, right):
    return lax.dot_general(left, right, (((0,), (0,)), ((), ())), preferred_element_type=jnp.float32)


def to_other_core(values):
    return lax.ppermute(values, "c", [(0, 1), (1, 0)])


def along_z(values, step):
    return lax.ppermute(values, Z, [(z, (z + step) % N_Z) for z in range(N_Z)])


def exchange(values, axis):
    return lax.all_to_all(values, axis, 0, 0, tiled=True)


def to_all(values, axis, count):
    return exchange(jnp.broadcast_to(values[None], (count,) + values.shape).reshape(-1, values.shape[1]), axis)


def per_device(features, weight, cotangent, tile_mask, row_codes, col_codes):
    x_hi, z_lo, core = lax.axis_index("xh"), lax.axis_index("zl"), lax.axis_index("c")
    subset = (lax.axis_index("xl") * N_Y + lax.axis_index("y")) * N_CORE + core

    threshold = (10 + 20 * subset // (N_REP - 1)) * hash_prime // 1000
    place = jnp.stack([core, x_hi, z_lo, threshold]).astype(jnp.int32)

    low, codes, shared = prepare(features, row_codes, col_codes, tile_mask)
    from_x = lax.ppermute(shared, "xh", [(0, 1), (1, 0)])
    block = lax.all_gather(low, "zh", axis=0, tiled=True)
    up, down = along_z(block, -1), along_z(block, 1)
    up, from_x, codes = lax.optimization_barrier((up, from_x, codes.astype(jnp.float32)))
    far = along_z(up, -1)
    own, cross, own_degree, cross_degree = build_adjacency(place, codes, from_x)
    gathered = jnp.concatenate([block, up, down, far], axis=0)
    gathered, own, cross, own_degree, cross_degree = lax.optimization_barrier(
        (gathered, own, cross, own_degree, cross_degree)
    )

    def with_degree(aggregate, degree):
        degree = jnp.pad(degree, ((0, 0), (0, 0), (0, F - 128)))
        return jnp.concatenate([aggregate.reshape(N_XY, RPD, F), degree], axis=1)

    crossing = to_other_core(with_degree(multiply(cross, gathered), cross_degree).astype(jnp.float16))
    aggregate, crossing = lax.optimization_barrier((multiply(own, gathered), crossing))
    sent = (with_degree(aggregate, own_degree) + crossing.astype(jnp.float32)).astype(jnp.float16)
    arrived = lax.all_to_all(sent, XY, 0, 0).astype(jnp.float32).sum(axis=0)
    degree = arrived[RPD, :RPD][:, None]
    aggregate = arrived[:RPD]

    row_scale = lax.rsqrt(1.0 + degree)
    hidden = (features + aggregate) * row_scale
    pre_act = jnp.dot(hidden, weight, precision=HIGH, preferred_element_type=jnp.float32)
    activated = jax.nn.softplus(pre_act)
    pulled = cotangent * jax.nn.sigmoid(pre_act) * row_scale

    pulled_block = to_all(pulled.astype(jnp.bfloat16), XY, N_XY)
    far_term = multiply_transposed(own[:, 3 * BLOCK :], pulled_block)
    term = multiply_transposed(own[:, : 3 * BLOCK], pulled_block)
    far_term, term, pulled_other = lax.optimization_barrier((far_term, term, to_other_core(pulled_block)))
    far_term += multiply_transposed(cross[:, 3 * BLOCK :], pulled_other)
    passed = along_z(far_term.astype(jnp.bfloat16), 1)
    term += multiply_transposed(cross[:, : 3 * BLOCK], pulled_other)
    down = along_z(term[2 * BLOCK :].astype(jnp.bfloat16), -1)
    up = along_z((term[BLOCK : 2 * BLOCK] + passed.astype(jnp.float32)).astype(jnp.bfloat16), 1)
    kept, ahead, opposite, behind = class_sums(lax.axis_index("zh"), term[:BLOCK], up, down)
    passed = along_z(opposite, N_Z_LO)
    down = along_z(behind, -N_Z_LO)
    up = along_z((ahead + passed.astype(jnp.float32)).astype(jnp.bfloat16), N_Z_LO)
    term = kept + up.astype(jnp.float32) + down.astype(jnp.float32)
    grad_input = lax.dot_general(
        pulled + term, weight, (((1,), (1,)), ((), ())), precision=HIGH, preferred_element_type=jnp.float32
    )
    return (activated, grad_input)


def solution(mesh):
    inner = Mesh(mesh.devices.reshape(N_Z_HI, N_Z_LO, N_X_HI, N_X_LO, N_Y, N_CORE), AXES)
    row, rep = ("zh", "zl", "xh"), ("xl", "y", "c")
    in_specs = (
        P(row + rep, None),
        P(),
        P(row + rep, None),
        P(row, rep),
        P(None, row),
        P(None, rep),
    )
    out_specs = (P(row + rep, None), P(row + rep, None))
    return jax.shard_map(per_device, mesh=inner, in_specs=in_specs, out_specs=out_specs, check_vma=False)
```

```python
import jax
import jax.numpy as jnp
from jax import lax
from jax.experimental import pallas as pl
from jax.experimental.pallas import tpu as pltpu
from jax.sharding import Mesh, PartitionSpec as P

HIGH = lax.Precision.HIGH
hash_prime = 65521
N_Z_HI, N_Z_LO, N_X_HI, N_X_LO, N_Y, N_CORE = 4, 4, 2, 2, 4, 2
N_Z = N_Z_HI * N_Z_LO
N_XY = N_X_HI * N_X_LO * N_Y
N_REP = N_X_LO * N_Y * N_CORE
RPD = 64
F = 512
R = N_XY * RPD
COLS = N_CORE * N_Z * RPD
HALF = COLS // 2
BLOCK = N_Z_HI * RPD
DIGITS = 16
AXES = ("zh", "zl", "xh", "xl", "y", "c")
Z = ("zh", "zl")
XY = ("xh", "xl", "y")


def centred(value):
    return value - jnp.round(value * (1.0 / hash_prime)) * float(hash_prime)


def two_digits(value):
    high = jnp.floor((value + 128.0) * (1.0 / 256.0))
    return value - 256.0 * high, high


def stack_rows(rows, width):
    row_index = lax.broadcasted_iota(jnp.int32, (DIGITS, width), 0)
    stacked = jnp.zeros((DIGITS, width), jnp.float32)
    for k, row in enumerate(rows):
        stacked = jnp.where(row_index == k, row, stacked)
    return stacked.astype(jnp.bfloat16)


def row_digits(first_code, second_code):
    digits = []
    for code in (first_code, second_code):
        for value in (code, centred(code * 256.0)):
            low, high = two_digits(value)
            digits.extend((low, 256.0 * high))
    low, high = two_digits(centred(centred((first_code + second_code) * 128.0) * 128.0))
    return digits + [low, 256.0 * high]


def column_digits(first_code, second_code):
    digits = []
    for code in (first_code, second_code):
        low, high = two_digits(code - 16384.0)
        digits.extend((low, low, high, high))
    return digits + [jnp.ones_like(first_code)] * 2


def halves(first, second, upper):
    lane = lax.broadcasted_iota(jnp.int32, first.shape, 1)
    lower_halves = jnp.where(lane < RPD, first, pltpu.roll(second, RPD, 1))
    upper_halves = jnp.where(lane < RPD, pltpu.roll(first, RPD, 1), second)
    return jnp.where(upper == 1, upper_halves, lower_halves)


def class_of(place, z_lo):
    return (z_lo + place + jnp.where(place == 2, 1, 0) - jnp.where(place == 3, 1, 0)) & (N_Z_LO - 1)


def adjacency_kernel(place_ref, codes_ref, from_x_ref, *refs):
    own_ref, cross_ref, own_degree_ref, cross_degree_ref, picked_ref, left_ref = refs
    core, x_hi, z_lo = place_ref[0], place_ref[1], place_ref[2]

    for crossed in range(2):
        for x in range(N_X_HI):
            for t in range(R // N_X_HI // 128):
                pieces = []
                for k in range(2):
                    at = pl.ds(256 * t + 128 * k, 128)
                    pieces.append(jnp.where(x_hi == x, codes_ref[:2, at], from_x_ref[:2, at]))
                picked_ref[:, pl.ds(R // N_X_HI * x + 128 * t, 128)] = halves(*pieces, core ^ crossed)
        rows = picked_ref[...].astype(jnp.float32)
        left_ref[crossed] = stack_rows(row_digits(rows[:1], rows[1:]), R)

    groups = (N_Z, HALF)
    column = lax.broadcasted_iota(jnp.int32, groups, 1)
    tile = ((column // RPD) & (N_Z_HI - 1)) * N_Z_LO + class_of(column // BLOCK, z_lo)
    spread = jnp.where(lax.broadcasted_iota(jnp.int32, groups, 0) == tile, 1.0, 0.0).astype(jnp.bfloat16)
    ones = jnp.ones((8, HALF), jnp.bfloat16)
    lane = lax.broadcasted_iota(jnp.int32, (8, 128), 1)
    for place in range(N_Z_LO):
        for h in range(N_Z_HI // 2):
            pieces = []
            for k in range(2):
                at = R + ((2 * h + k) * N_Z_LO + class_of(jnp.int32(place), z_lo)) * 128
                pieces.append(codes_ref[:2, pl.ds(pl.multiple_of(at, 128), 128)])
            picked_ref[:, pl.ds(BLOCK * place + 128 * h, 128)] = halves(*pieces, x_hi)
    columns = picked_ref[...].astype(jnp.float32)
    right = stack_rows(column_digits(columns[:1], columns[1:]), HALF)
    masks = (codes_ref[:, R + COLS : R + COLS + N_Z], from_x_ref[:, R : R + N_Z])
    mask = jnp.concatenate([jnp.where(x_hi == x, *masks) for x in range(N_X_HI)], axis=0)
    mask = mask.astype(jnp.float32).astype(jnp.bfloat16)
    threshold = place_ref[3].astype(jnp.float32)
    middle = (threshold - 1.0) * 0.5
    reach = jnp.dot(mask, spread, preferred_element_type=jnp.float32) * (threshold * 0.5)

    for crossed, (block_ref, degree_ref) in enumerate(((own_ref, own_degree_ref), (cross_ref, cross_degree_ref))):
        for pair in range(N_XY // 2):
            at = pl.ds(2 * RPD * pair, 2 * RPD)
            contract = (((0,), (0,)), ((), ()))
            value = lax.dot_general(left_ref[crossed, :, at], right, contract, preferred_element_type=jnp.float32)
            nearest = jnp.round(value * (1.0 / hash_prime))
            residue = value - nearest * float(hash_prime)
            kept = []
            for k in range(2):
                part = residue[k * RPD : (k + 1) * RPD]
                inside = jnp.abs(part - middle) < reach[2 * pair + k][None, :]
                kept.append(jnp.where(inside, 1.0, 0.0))
            low = jnp.concatenate(kept, axis=0).astype(jnp.bfloat16)
            block_ref[at, :] = low
            contract = (((1,), (1,)), ((), ()))
            count = lax.dot_general(ones, low, contract, preferred_element_type=jnp.float32)
            for k in range(2):
                part = pltpu.roll(count, RPD, 1) if k else count
                degree_ref[2 * pair + k] = jnp.where(lane < RPD, part, 0.0)


def build_adjacency(place, codes, from_x):
    vmem = pl.BlockSpec(memory_space=pltpu.VMEM)
    block = jax.ShapeDtypeStruct((R, HALF), jnp.bfloat16)
    degree = jax.ShapeDtypeStruct((N_XY, 8, 128), jnp.float32)
    return pl.pallas_call(
        adjacency_kernel,
        in_specs=[pl.BlockSpec(memory_space=pltpu.SMEM), vmem, vmem],
        out_specs=[vmem] * 4,
        out_shape=[block, block, degree, degree],
        scratch_shapes=[pltpu.VMEM((2, R), jnp.int32), pltpu.VMEM((2, DIGITS, R), jnp.bfloat16)],
        compiler_params=pltpu.CompilerParams(vmem_limit_bytes=6 * 1024 * 1024),
        cost_estimate=pl.CostEstimate(flops=4 * R * HALF * 16, bytes_accessed=4 * R * HALF, transcendentals=0),
    )(place, codes, from_x)


def prepare_kernel(features_ref, rows_ref, columns_ref, mask_ref, low_ref, codes_ref, shared_ref, *scratch):
    values_ref, *held, sems = scratch
    copies = [
        pltpu.make_async_copy(source, target, sems.at[k])
        for k, (source, target) in enumerate(zip((features_ref, rows_ref, columns_ref, mask_ref), (values_ref, *held)))
    ]
    for copy in copies:
        copy.start()
    codes_ref[...] = jnp.zeros_like(codes_ref)
    shared_ref[...] = jnp.zeros_like(shared_ref)
    for copy in copies:
        copy.wait()
    rows, columns, mask = held
    codes_ref[:2, :R] = rows[...]
    codes_ref[:2, R : R + COLS] = columns[...]
    codes_ref[:, R + COLS : R + COLS + N_Z] = mask[...]
    shared_ref[:2, :R] = rows[...]
    shared_ref[:, R : R + N_Z] = mask[...]
    low_ref[...] = values_ref[...].astype(jnp.bfloat16)


def prepare(features, row_codes, col_codes, tile_mask):
    vmem = pl.BlockSpec(memory_space=pltpu.VMEM)
    arrays = (features, row_codes, col_codes, tile_mask)
    return pl.pallas_call(
        prepare_kernel,
        in_specs=[pl.BlockSpec(memory_space=pl.ANY)] * 4,
        out_specs=[vmem, vmem, vmem],
        out_shape=[
            jax.ShapeDtypeStruct(features.shape, jnp.bfloat16),
            jax.ShapeDtypeStruct((8, R + COLS + 128), jnp.int32),
            jax.ShapeDtypeStruct((8, R + 128), jnp.int32),
        ],
        scratch_shapes=[pltpu.VMEM(array.shape, array.dtype) for array in arrays] + [pltpu.SemaphoreType.DMA((4,))],
        compiler_params=pltpu.CompilerParams(vmem_limit_bytes=56 * 1024 * 1024),
    )(*arrays)


def class_sums_kernel(z_hi_ref, term_ref, up_ref, down_ref, *sum_refs):
    for step, sum_ref in enumerate(sum_refs):
        start = ((z_hi_ref[0] + step) & (N_Z_HI - 1)) * RPD
        at = pl.ds(pl.multiple_of(start, RPD), RPD)
        total = term_ref[at, :] + up_ref[at, :].astype(jnp.float32) + down_ref[at, :].astype(jnp.float32)
        sum_ref[...] = total.astype(sum_ref.dtype)


def class_sums(z_hi, term, up, down):
    vmem = pl.BlockSpec(memory_space=pltpu.VMEM)
    kinds = (jnp.float32, jnp.float32, jnp.bfloat16, jnp.bfloat16)
    return pl.pallas_call(
        class_sums_kernel,
        in_specs=[pl.BlockSpec(memory_space=pltpu.SMEM), vmem, vmem, vmem],
        out_specs=[vmem] * N_Z_HI,
        out_shape=[jax.ShapeDtypeStruct((RPD, F), kind) for kind in kinds],
        compiler_params=pltpu.CompilerParams(vmem_limit_bytes=4 * 1024 * 1024),
    )(z_hi.reshape(1).astype(jnp.int32), term, up, down)


def multiply(left, right):
    return jnp.dot(left, right, preferred_element_type=jnp.float32)


def multiply_transposed(left, right):
    return lax.dot_general(left, right, (((0,), (0,)), ((), ())), preferred_element_type=jnp.float32)


def to_other_core(values):
    return lax.ppermute(values, "c", [(0, 1), (1, 0)])


def along_z(values, step):
    return lax.ppermute(values, Z, [(z, (z + step) % N_Z) for z in range(N_Z)])


def exchange(values, axis):
    return lax.all_to_all(values, axis, 0, 0, tiled=True)


def to_all(values, axis, count):
    return exchange(jnp.broadcast_to(values[None], (count,) + values.shape).reshape(-1, values.shape[1]), axis)


def per_device(features, weight, cotangent, tile_mask, row_codes, col_codes):
    x_hi, z_lo, core = lax.axis_index("xh"), lax.axis_index("zl"), lax.axis_index("c")
    subset = (lax.axis_index("xl") * N_Y + lax.axis_index("y")) * N_CORE + core

    threshold = (10 + 20 * subset // (N_REP - 1)) * hash_prime // 1000
    place = jnp.stack([core, x_hi, z_lo, threshold]).astype(jnp.int32)

    low, codes, shared = prepare(features, row_codes, col_codes, tile_mask)
    from_x = lax.ppermute(shared, "xh", [(0, 1), (1, 0)])
    block = lax.all_gather(low, "zh", axis=0, tiled=True)
    up, down = along_z(block, -1), along_z(block, 1)
    up, from_x = lax.optimization_barrier((up, from_x))
    far = along_z(up, -1)
    own, cross, own_degree, cross_degree = build_adjacency(place, codes, from_x)
    gathered = jnp.concatenate([block, up, down, far], axis=0)
    gathered, own, cross, own_degree, cross_degree = lax.optimization_barrier(
        (gathered, own, cross, own_degree, cross_degree)
    )

    def with_degree(aggregate, degree):
        degree = jnp.pad(degree, ((0, 0), (0, 0), (0, F - 128)))
        return jnp.concatenate([aggregate.reshape(N_XY, RPD, F), degree], axis=1)

    crossing = to_other_core(with_degree(multiply(cross, gathered), cross_degree).astype(jnp.float16))
    aggregate, crossing = lax.optimization_barrier((multiply(own, gathered), crossing))
    sent = (with_degree(aggregate, own_degree) + crossing.astype(jnp.float32)).astype(jnp.float16)
    arrived = lax.all_to_all(sent, XY, 0, 0).astype(jnp.float32).sum(axis=0)
    degree = arrived[RPD, :RPD][:, None]
    aggregate = arrived[:RPD]

    row_scale = lax.rsqrt(1.0 + degree)
    hidden = (features + aggregate) * row_scale
    pre_act = jnp.dot(hidden, weight, precision=HIGH, preferred_element_type=jnp.float32)
    activated = jax.nn.softplus(pre_act)
    pulled = cotangent * jax.nn.sigmoid(pre_act) * row_scale

    pulled_block = to_all(pulled.astype(jnp.bfloat16), XY, N_XY)
    far_term = multiply_transposed(own[:, 3 * BLOCK :], pulled_block)
    term = multiply_transposed(own[:, : 3 * BLOCK], pulled_block)
    far_term, term, pulled_other = lax.optimization_barrier((far_term, term, to_other_core(pulled_block)))
    far_term += multiply_transposed(cross[:, 3 * BLOCK :], pulled_other)
    passed = along_z(far_term.astype(jnp.bfloat16), 1)
    term += multiply_transposed(cross[:, : 3 * BLOCK], pulled_other)
    down = along_z(term[2 * BLOCK :].astype(jnp.bfloat16), -1)
    up = along_z((term[BLOCK : 2 * BLOCK] + passed.astype(jnp.float32)).astype(jnp.bfloat16), 1)
    kept, ahead, opposite, behind = class_sums(lax.axis_index("zh"), term[:BLOCK], up, down)
    passed = along_z(opposite, N_Z_LO)
    down = along_z(behind, -N_Z_LO)
    up = along_z((ahead + passed.astype(jnp.float32)).astype(jnp.bfloat16), N_Z_LO)
    term = kept + up.astype(jnp.float32) + down.astype(jnp.float32)
    grad_input = lax.dot_general(
        pulled + term, weight, (((1,), (1,)), ((), ())), precision=HIGH, preferred_element_type=jnp.float32
    )
    return (activated, grad_input)


def solution(mesh):
    inner = Mesh(mesh.devices.reshape(N_Z_HI, N_Z_LO, N_X_HI, N_X_LO, N_Y, N_CORE), AXES)
    row, rep = ("zh", "zl", "xh"), ("xl", "y", "c")
    in_specs = (
        P(row + rep, None),
        P(),
        P(row + rep, None),
        P(row, rep),
        P(None, row),
        P(None, rep),
    )
    out_specs = (P(row + rep, None), P(row + rep, None))
    return jax.shard_map(per_device, mesh=inner, in_specs=in_specs, out_specs=out_specs, check_vma=False)
```
